32 devices in a mesh: row: 4 (over y, core), col: 8 (over z, x).
Axes of the slice: x: 2, y: 2, z: 4, core: 2. Of those that a mesh axis runs over, the one named last changes fastest.
Arguments:
- fields: float32 [4096, 5, 4096], P(('row', 'col')), as said below
- counts: int32 [4, 8], P('row', 'col'), may hold values from 1 to 128, 512 in all within a row
Outputs:
- fields_out: float32 [4096, 5, 4096], P(('row', 'col'))
The draws below stay inside these ranges and needn't reach their ends.
Inputs may be any that keep to these rules, and one draw needn't show every extreme that they name: `fields`: in every slot, also those that hold no patch, density lies in 0.5 to 3, pressure 0.4 (E - |m|^2 / (2 rho)) in 0.5 to 2 and each velocity component in -0.5 to 0.5. Each index of row holds 512 patches in all: the entries of counts[r] sum to 512, and some device of each index of row holds 128.
All inputs are finite; a program needn't handle non-finite values.
Results may differ from the reference program's by a relative error of at most 0.0003.
Values sent between devices are 32-bit elements; how exact they have to be, the bound alone decides.
A program may use at most 192 MiB of HBM per device.

```python
import math
import jax
import jax.numpy as jnp
import numpy as np
from jax import lax

PE = 16
GX = 256
GY = 256
GZ = 128
LXR = 4
LY = 16
LZ = 8
PPR = 512
CAP = 128
SLOTS = 4096
CELLS = 4096
N_ROW = 4
N_COL = 8


def draw_fields(key, part):
    subkeys = jax.random.split(key, 3)
    slot_shape = (SLOTS, CELLS)
    density = jnp.exp(jax.random.uniform(subkeys[0], slot_shape, minval=math.log(0.5), maxval=math.log(2.0)))
    velocity = jax.random.uniform(subkeys[1], (3,) + slot_shape, minval=-0.5, maxval=0.5)
    pressure = jnp.exp(jax.random.uniform(subkeys[2], slot_shape, minval=math.log(0.5), maxval=math.log(2.0)))
    momenta = density[None] * velocity
    speed_sq = velocity[0] * velocity[0] + velocity[1] * velocity[1] + velocity[2] * velocity[2]
    energy = pressure / 0.4 + 0.5 * density * speed_sq
    return jnp.stack([density, momenta[0], momenta[1], momenta[2], energy], axis=1).astype(jnp.float32)


def split_up(count, total, reach, slope):
    weights = [(1 << 20) // math.isqrt(grade ** slope) + 1 for grade in range(2, count + 1)]
    spare, holding = total - reach - (count - 1), [1] * (count - 1)
    while spare > 0:
        movable = [i for i in range(count - 1) if holding[i] < reach]
        mass, remaining = sum([weights[i] for i in movable]), spare
        for i in movable:
            more = min(reach - holding[i], max(1, remaining * weights[i] // mass), spare)
            holding[i] = holding[i] + more
            spare = spare - more
    return np.array([reach] + holding)


def uneven_parts(key, number_of, total, most, slope):
    if number_of == 2:
        one = jax.random.randint(key, (), max(1, total - most), min(most, total - 1) + 1)
        return jnp.stack([one, total - one])
    sizes = jnp.asarray(split_up(number_of, total, most, slope), jnp.int32)
    twos = (number_of - 1) // 2
    source_of, receiver = sizes[1:1 + 2 * twos:2], sizes[2:2 + 2 * twos:2]
    slack = jnp.minimum(source_of - 1, most - receiver)
    shifted = jax.random.randint(jax.random.fold_in(key, 1), (twos,), 0, 1 << 20) % (slack + 1)
    sizes = sizes.at[1:1 + 2 * twos:2].set(source_of - shifted).at[2:2 + 2 * twos:2].set(receiver + shifted)
    return sizes[jax.random.permutation(jax.random.fold_in(key, 2), number_of)]


def setup_inputs(seed: int = 0) -> dict:
    seeds = jax.random.split(jax.random.key(seed), 3)
    return {
        "fields": draw_fields(jax.random.fold_in(seeds[2], 71), 0),
        "counts": jax.vmap(lambda own: uneven_parts(own, N_COL, PPR, CAP, 2))(jax.random.split(seeds[1], N_ROW)).reshape((N_ROW, N_COL)).astype(jnp.int32),
    }


gamma_gas = 1.4
speed_bound = 4.0
time_step = 0.03
four_pi_g = 10.0


def minmod_slope(lower_gap, upper_gap):
    return 0.5 * (jnp.sign(lower_gap) + jnp.sign(upper_gap)) * jnp.minimum(jnp.abs(lower_gap), jnp.abs(upper_gap))


def normal_flux(states, direction):
    density = states[0]
    momenta = states[1:4]
    energy = states[4]
    velocity = momenta[direction] / density
    kinetic = 0.5 * (momenta[0] * momenta[0] + momenta[1] * momenta[1] + momenta[2] * momenta[2]) / density
    pressure = (gamma_gas - 1.0) * (energy - kinetic)
    pieces = [momenta[direction]]
    for component in range(3):
        flux_term = momenta[component] * velocity
        if component == direction:
            flux_term = flux_term + pressure
        pieces.append(flux_term)
    pieces.append((energy + pressure) * velocity)
    return jnp.stack(pieces)


def cut_range(array, dim_index, first_cell, count_cells):
    return lax.slice_in_dim(array, first_cell, first_cell + count_cells, axis=dim_index)


def face_rates(states):
    total_rate = None
    for direction in range(3):
        dim_index = direction + 1
        trimmed = states
        for other_dim in range(1, 4):
            if other_dim != dim_index:
                trimmed = cut_range(trimmed, other_dim, 2, trimmed.shape[other_dim] - 4)
        length = trimmed.shape[dim_index]
        lower_cell = cut_range(trimmed, dim_index, 0, length - 3)
        centre = cut_range(trimmed, dim_index, 1, length - 3)
        upper_cell = cut_range(trimmed, dim_index, 2, length - 3)
        far_cell = cut_range(trimmed, dim_index, 3, length - 3)
        left_state = centre + 0.5 * minmod_slope(centre - lower_cell, upper_cell - centre)
        right_state = upper_cell - 0.5 * minmod_slope(upper_cell - centre, far_cell - upper_cell)
        face_flux = 0.5 * (normal_flux(left_state, direction) + normal_flux(right_state, direction)) - 0.5 * speed_bound * (right_state - left_state)
        change = cut_range(face_flux, dim_index, 1, length - 4) - cut_range(face_flux, dim_index, 0, length - 4)
        total_rate = change if total_rate is None else total_rate + change
    return -total_rate


def crop_all(array, margin):
    return array[:, margin:array.shape[1] - margin, margin:array.shape[2] - margin, margin:array.shape[3] - margin]


def advance(extended):
    first = crop_all(extended, 2) + time_step * face_rates(extended)
    second = crop_all(first, 2) + time_step * face_rates(first)
    return 0.5 * crop_all(extended, 4) + 0.5 * second


def lap_eigen(wave, length):
    return 2.0 * jnp.cos((2.0 * math.pi / length) * wave) - 2.0


def apply_kick(stepped, gradient):
    density = stepped[0]
    momenta = stepped[1:4]
    new_momenta = momenta - time_step * density[None] * gradient
    work_done = momenta[0] * gradient[0] + momenta[1] * gradient[1] + momenta[2] * gradient[2]
    new_energy = stepped[4] - time_step * work_done
    return jnp.concatenate([stepped[0:1], new_momenta, new_energy[None]], axis=0)


def reference(fields, counts):
    counts = counts.astype(jnp.int32)
    starts = (jnp.cumsum(counts, axis=1) - counts).astype(jnp.int32)
    positions = jnp.arange(PPR, dtype=jnp.int32)
    owners = (jnp.sum((starts[:, None, :] <= positions[None, :, None]).astype(jnp.int32), axis=2) - 1).astype(jnp.int32)
    owner_start = jnp.take_along_axis(starts, owners, axis=1).astype(jnp.int32)
    row_ids = jnp.arange(N_ROW, dtype=jnp.int32)
    slot_rows = ((row_ids[:, None] * N_COL + owners) * CAP + positions[None, :] - owner_start).astype(jnp.int32)
    patches = jnp.take(fields, slot_rows.reshape(-1), axis=0)
    state = patches.reshape(N_ROW, LXR, LZ, LY, 5, PE, PE, PE).transpose(4, 0, 1, 5, 3, 6, 2, 7).reshape(5, GX, GY, GZ)

    padded = jnp.pad(state, ((0, 0), (4, 4), (4, 4), (4, 4)), mode="wrap")
    slab_width = GX // N_ROW

    def one_slab(slab_index):
        slab_piece = lax.dynamic_slice_in_dim(padded, slab_index * slab_width, slab_width + 8, axis=1)
        return advance(slab_piece)

    slab_results = lax.map(one_slab, jnp.arange(N_ROW, dtype=jnp.int32))
    stepped = jnp.moveaxis(slab_results, 0, 1).reshape(5, GX, GY, GZ)

    spectrum = jnp.fft.fftn(stepped[0])
    wave_x = jnp.arange(GX, dtype=jnp.float32)
    wave_y = jnp.arange(GY, dtype=jnp.float32)
    wave_z = jnp.arange(GZ, dtype=jnp.float32)
    eigen = (lap_eigen(wave_x, GX)[:, None, None] + lap_eigen(wave_y, GY)[None, :, None]) + lap_eigen(wave_z, GZ)[None, None, :]
    zero_mode = (wave_x == 0.0)[:, None, None] & (wave_y == 0.0)[None, :, None] & (wave_z == 0.0)[None, None, :]
    green = jnp.where(zero_mode, 0.0, four_pi_g / jnp.where(zero_mode, -1.0, eigen))
    potential = jnp.real(jnp.fft.ifftn(spectrum * green))
    gradient = jnp.stack([0.5 * (jnp.roll(potential, -1, direction) - jnp.roll(potential, 1, direction)) for direction in range(3)])
    kicked = apply_kick(stepped, gradient)

    out_patches = kicked.reshape(5, N_ROW, LXR, PE, LY, PE, LZ, PE).transpose(1, 2, 6, 4, 0, 3, 5, 7).reshape(N_ROW * PPR, 5, CELLS)
    slot_ids = jnp.arange(SLOTS, dtype=jnp.int32)
    row_of = (slot_ids // (N_COL * CAP)).astype(jnp.int32)
    col_of = ((slot_ids // CAP) % N_COL).astype(jnp.int32)
    within = (slot_ids % CAP).astype(jnp.int32)
    slot_counts = counts[row_of, col_of]
    slot_starts = starts[row_of, col_of]
    live = within < slot_counts
    source = (row_of * PPR + jnp.where(live, slot_starts + within, 0)).astype(jnp.int32)
    return jnp.where(live[:, None, None], jnp.take(out_patches, source, axis=0), 0.0)
```

```python
import functools
import math

import jax
import jax.numpy as jnp
import numpy as np
from jax import lax
from jax.experimental import pallas as pl
from jax.experimental.pallas import tpu as pltpu
from jax.sharding import PartitionSpec as P

PE = 16
GX = 256
GY = 256
GZ = 128
LANES = 128
SUB = 8
VMEM_BYTES = 56 * 1024 * 1024


gamma_gas = 1.4
speed_bound = 4.0
time_step = 0.03
four_pi_g = 10.0


def shift_pair(axis):
    count = lax.axis_size(axis)
    forward = [(i, (i + 1) % count) for i in range(count)]
    backward = [(target, source) for source, target in forward]
    return forward, backward


def edges(block, axis, dim, width):
    forward, backward = shift_pair(axis)
    low = lax.ppermute(
        lax.slice_in_dim(block, block.shape[dim] - width, None, axis=dim), axis, forward
    )
    high = lax.ppermute(lax.slice_in_dim(block, 0, width, axis=dim), axis, backward)
    return low, high


def padded(block, sides, width):
    for axis, dim in sides:
        low, high = edges(block, axis, dim, width)
        block = jnp.concatenate([low, block, high], axis=dim)
    return block


def half_flux(state, direction):
    density, momenta, energy = state[0], state[1:4], state[4]
    inverse = 1.0 / density
    velocity = momenta[direction] * inverse
    kinetic = (
        0.5
        * (momenta[0] * momenta[0] + momenta[1] * momenta[1] + momenta[2] * momenta[2])
        * inverse
    )
    pressure = (gamma_gas - 1.0) * (energy - kinetic)
    half_velocity = 0.5 * velocity
    pieces = [0.5 * momenta[direction]]
    for component in range(3):
        term = momenta[component] * half_velocity
        if component == direction:
            term = term + 0.5 * pressure
        pieces.append(term)
    pieces.append((energy + pressure) * half_velocity)
    return pieces


def side_terms(lower_gap, centre, upper_gap, direction):
    left, right = [], []
    for low, mid, high in zip(lower_gap, centre, upper_gap):
        slope = jnp.maximum(jnp.minimum(low, high), 0.0) + jnp.minimum(
            jnp.maximum(low, high), 0.0
        )
        left.append(mid + 0.5 * slope)
        right.append(mid - 0.5 * slope)
    damping = 0.5 * speed_bound
    below = [f + damping * u for f, u in zip(half_flux(left, direction), left)]
    above = [f - damping * u for f, u in zip(half_flux(right, direction), right)]
    return below, above


def step_kernel(ext_ref, out_ref, first_ref, part_ref, last_ref):
    planes = ext_ref.shape[1]
    depth_y = ext_ref.shape[2]
    out_y = out_ref.shape[2]

    def plane(ref, i):
        return [ref[q, i] for q in range(5)]

    def x_terms(ref, i):
        low, mid, high = plane(ref, i - 1), plane(ref, i), plane(ref, i + 1)
        return side_terms(
            [m - l for l, m in zip(low, mid)], mid, [h - m for m, h in zip(mid, high)], 0
        )

    def begin(ref, i):
        before, _ = x_terms(ref, i - 1)
        below, above = x_terms(ref, i)
        for q in range(5):
            last_ref[q] = below[q]
            part_ref[q] = below[q] - above[q] - before[q]

    def change(ref, i):
        below, above = x_terms(ref, i + 1)
        total = []
        for q in range(5):
            total.append(part_ref[q] + above[q])
            part_ref[q] = below[q] - above[q] - last_ref[q]
            last_ref[q] = below[q]
        mid = plane(ref, i)
        for direction, axis, size in ((1, 0, depth_y), (2, 1, LANES)):
            upper_gap = [pltpu.roll(m, size - 1, axis) - m for m in mid]
            lower_gap = [pltpu.roll(g, 1, axis) for g in upper_gap]
            below, above = side_terms(lower_gap, mid, upper_gap, direction)
            total = [
                t + (b - a) + (pltpu.roll(a, size - 1, axis) - pltpu.roll(b, 1, axis))
                for t, b, a in zip(total, below, above)
            ]
        return mid, total

    begin(ext_ref, 2)

    def first_step(i, carry):
        mid, total = change(ext_ref, i)
        for q in range(5):
            first_ref[q, i] = mid[q] - time_step * total[q]
        return carry

    lax.fori_loop(2, planes - 2, first_step, 0)
    begin(first_ref, 4)

    def second_step(i, carry):
        mid, total = change(first_ref, i)
        for q in range(5):
            value = 0.5 * ext_ref[q, i] + 0.5 * (mid[q] - time_step * total[q])
            out_ref[q, i - 4] = pltpu.roll(value, depth_y - 4, 0)[:out_y]
        return carry

    lax.fori_loop(4, planes - 4, second_step, 0)


def advance(extended):
    _, planes, depth_y, depth_z = extended.shape
    out_shape = (5, planes - 8, depth_y - 8, depth_z)
    cells = planes * depth_y * depth_z
    return pl.pallas_call(
        step_kernel,
        out_shape=jax.ShapeDtypeStruct(out_shape, jnp.float32),
        in_specs=[pl.BlockSpec(memory_space=pltpu.VMEM)],
        out_specs=pl.BlockSpec(memory_space=pltpu.VMEM),
        scratch_shapes=[
            pltpu.VMEM((5, planes, depth_y, depth_z), jnp.float32),
            pltpu.VMEM((5, depth_y, depth_z), jnp.float32),
            pltpu.VMEM((5, depth_y, depth_z), jnp.float32),
        ],
        compiler_params=pltpu.CompilerParams(vmem_limit_bytes=VMEM_BYTES),
        cost_estimate=pl.CostEstimate(
            flops=900 * cells, bytes_accessed=40 * cells, transcendentals=0
        ),
        name="gas_step",
    )(extended)


def pack_kernel(block_y, brick_y, start_ref, in_ref, out_ref):
    cols_count, _, repeat_y = out_ref.shape[:3]
    halves = brick_y // SUB
    per_patch = PE // brick_y
    stride = PE * halves
    lat_y = in_ref.shape[0]
    offset = lax.rem(start_ref[0], lat_y)

    def one(i, carry):
        peer = i // repeat_y
        inner = lax.rem(i, repeat_y)
        y_patch = peer * block_y // PE + inner
        slot = lax.rem(y_patch - offset + lat_y, lat_y)
        brick = lax.rem(peer, per_patch)
        for row in range(stride):
            a, half = divmod(row, halves)
            lane = (2 * a + half) * LANES
            if per_patch > 1:
                lane = pl.multiple_of(lane + brick * halves * LANES, LANES)
            out_ref[peer, 0, inner, pl.ds(row, 5, stride=stride), :] = in_ref[
                slot, :, pl.ds(lane, LANES)
            ]
        return carry

    lax.fori_loop(0, cols_count * repeat_y, one, 0)


def pack_slots(fields, own_start, cols_count, block_y, brick_y, lat_y, repeat_y):
    capacity = fields.shape[0]
    groups = capacity // lat_y
    rows = 5 * PE * (brick_y // SUB)
    return pl.pallas_call(
        functools.partial(pack_kernel, block_y, brick_y),
        out_shape=jax.ShapeDtypeStruct(
            (cols_count, groups, repeat_y, rows, LANES), jnp.float32
        ),
        grid_spec=pltpu.PrefetchScalarGridSpec(
            num_scalar_prefetch=1,
            grid=(groups,),
            in_specs=[pl.BlockSpec((lat_y, 5, PE * PE * PE), lambda g, s: (g, 0, 0))],
            out_specs=pl.BlockSpec(
                (cols_count, 1, repeat_y, rows, LANES), lambda g, s: (0, g, 0, 0, 0)
            ),
        ),
        compiler_params=pltpu.CompilerParams(vmem_limit_bytes=VMEM_BYTES),
        name="pack_slots",
    )(own_start.reshape(1), fields)


def unpack_kernel(block_y, brick_y, info_ref, in_ref, out_ref):
    repeat_y = in_ref.shape[2]
    halves = brick_y // SUB
    per_patch = PE // brick_y
    stride = PE * halves
    lat_y = out_ref.shape[0]
    base = pl.program_id(0) * lat_y

    def one(t, carry):
        y_patch = lax.rem(info_ref[0] + t, lat_y)
        live = jnp.full((5, LANES), base + t, jnp.int32) < info_ref[1]
        inner = lax.rem(y_patch, repeat_y)
        for brick in range(per_patch):
            peer = (y_patch * PE + brick * brick_y) // block_y
            for row in range(stride):
                a, half = divmod(row, halves)
                lane = (2 * a + brick * halves + half) * LANES
                value = in_ref[peer, 0, inner, pl.ds(row, 5, stride=stride), :]
                out_ref[t, :, pl.ds(lane, LANES)] = jnp.where(live, value, 0.0)
        return carry

    lax.fori_loop(0, lat_y, one, 0)


def unpack_slots(arrived, own_start, own_count, block_y, brick_y, lat_y):
    cols_count, groups, repeat_y, rows, _ = arrived.shape
    return pl.pallas_call(
        functools.partial(unpack_kernel, block_y, brick_y),
        out_shape=jax.ShapeDtypeStruct((groups * lat_y, 5, PE * PE * PE), jnp.float32),
        grid_spec=pltpu.PrefetchScalarGridSpec(
            num_scalar_prefetch=1,
            grid=(groups,),
            in_specs=[
                pl.BlockSpec(
                    (cols_count, 1, repeat_y, rows, LANES), lambda g, s: (0, g, 0, 0, 0)
                )
            ],
            out_specs=pl.BlockSpec((lat_y, 5, PE * PE * PE), lambda g, s: (g, 0, 0)),
        ),
        compiler_params=pltpu.CompilerParams(vmem_limit_bytes=VMEM_BYTES),
        name="unpack_slots",
    )(jnp.stack([own_start, own_count]), arrived)


def swap_blocks(values):
    lane = lax.broadcasted_iota(jnp.int32, (SUB, LANES), 1)
    count = len(values)
    step = 1
    while step < count:
        shift = step * PE
        low = (lane // shift) % 2 == 0
        swapped = list(values)
        for i in range(count):
            if i & step == 0:
                one, two = values[i], values[i | step]
                swapped[i] = jnp.where(low, one, pltpu.roll(two, shift, 1))
                swapped[i | step] = jnp.where(low, pltpu.roll(one, LANES - shift, 1), two)
        values = swapped
        step *= 2
    return values


def gather_kernel(index_ref, *refs):
    lat_z = GZ // PE
    in_refs, out_ref, rows_ref = refs[:lat_z], refs[lat_z], refs[lat_z + 1]
    brick_y = out_ref.shape[3]
    groups = in_refs[0].shape[1] // SUB

    def regroup(m, carry):
        at = pl.multiple_of(m * SUB, SUB)
        values = swap_blocks([ref[0, pl.ds(at, SUB), :] for ref in in_refs])
        for b in range(SUB):
            rows_ref[pl.ds(m * (SUB * SUB) + b, SUB, stride=SUB), :] = values[b]
        return carry

    lax.fori_loop(0, groups, regroup, 0)
    for q in range(5):

        def place(a, carry):
            at = pl.multiple_of((q * PE + a) * brick_y, SUB)
            out_ref[q, a, 0] = rows_ref[pl.ds(at, brick_y), :]
            return carry

        lax.fori_loop(0, PE, place, 0)


def gather_bricks(arrived, source_index, lat_x, per_pencil_y, brick_y):
    lat_z = GZ // PE
    rows = arrived.shape[1]

    def picked(zl):
        return lambda i, w, index: (index[(i * per_pencil_y + w) * lat_z + zl], 0, 0)

    out = pl.pallas_call(
        gather_kernel,
        out_shape=jax.ShapeDtypeStruct(
            (5, lat_x * PE, per_pencil_y, brick_y, LANES), jnp.float32
        ),
        grid_spec=pltpu.PrefetchScalarGridSpec(
            num_scalar_prefetch=1,
            grid=(lat_x, per_pencil_y),
            in_specs=[pl.BlockSpec((1, rows, LANES), picked(zl)) for zl in range(lat_z)],
            out_specs=pl.BlockSpec(
                (5, PE, 1, brick_y, LANES), lambda i, w, index: (0, i, w, 0, 0)
            ),
            scratch_shapes=[pltpu.VMEM((rows * SUB, LANES), jnp.float32)],
        ),
        compiler_params=pltpu.CompilerParams(vmem_limit_bytes=VMEM_BYTES),
        name="gather_bricks",
    )(source_index, *([arrived] * lat_z))
    return out.reshape(5, lat_x * PE, per_pencil_y * brick_y, GZ)


def kick_kernel(index_ref, state_ref, gradient_ref, out_ref, rows_ref, brick_ref, sems):
    lat_z = GZ // PE
    brick_y = state_ref.shape[3]
    groups = brick_ref.shape[1] // SUB
    at_grid = (pl.program_id(0) * pl.num_programs(1) + pl.program_id(1)) * lat_z

    def kick(a, carry):
        density = state_ref[0, a, 0]
        momenta = [state_ref[1 + d, a, 0] for d in range(3)]
        slopes = [gradient_ref[d, a, 0] for d in range(3)]
        work = momenta[0] * slopes[0] + momenta[1] * slopes[1] + momenta[2] * slopes[2]
        pieces = [density]
        for d in range(3):
            pieces.append(momenta[d] - time_step * density * slopes[d])
        pieces.append(state_ref[4, a, 0] - time_step * work)
        for q in range(5):
            at = pl.multiple_of((q * PE + a) * brick_y, SUB)
            rows_ref[pl.ds(at, brick_y), :] = pieces[q]
        return carry

    lax.fori_loop(0, PE, kick, 0)

    def regroup(m, carry):
        at = pl.multiple_of(m * SUB, SUB)
        values = swap_blocks(
            [rows_ref[pl.ds(m * (SUB * SUB) + b, SUB, stride=SUB), :] for b in range(SUB)]
        )
        for zl in range(lat_z):
            brick_ref[zl, pl.ds(at, SUB), :] = values[zl]
        return carry

    lax.fori_loop(0, groups, regroup, 0)
    copies = [
        pltpu.make_async_copy(
            brick_ref.at[zl], out_ref.at[index_ref[at_grid + zl]], sems.at[zl]
        )
        for zl in range(lat_z)
    ]
    for copy in copies:
        copy.start()
    for copy in copies:
        copy.wait()


def kick_bricks(stepped, gradient, source_index, buffer_rows, lat_x, per_pencil_y, brick_y):
    lat_z = GZ // PE
    rows = 5 * PE * (brick_y // SUB)
    shape = (lat_x * PE, per_pencil_y, brick_y, GZ)

    def block(count):
        return pl.BlockSpec((count, PE, 1, brick_y, GZ), lambda i, w, index: (0, i, w, 0, 0))

    return pl.pallas_call(
        kick_kernel,
        out_shape=jax.ShapeDtypeStruct((buffer_rows, rows, LANES), jnp.float32),
        grid_spec=pltpu.PrefetchScalarGridSpec(
            num_scalar_prefetch=1,
            grid=(lat_x, per_pencil_y),
            in_specs=[block(5), block(3)],
            out_specs=pl.BlockSpec(memory_space=pl.ANY),
            scratch_shapes=[
                pltpu.VMEM((rows * SUB, LANES), jnp.float32),
                pltpu.VMEM((lat_z, rows, LANES), jnp.float32),
                pltpu.SemaphoreType.DMA((lat_z,)),
            ],
        ),
        compiler_params=pltpu.CompilerParams(vmem_limit_bytes=VMEM_BYTES),
        name="kick_bricks",
    )(source_index, stepped.reshape((5,) + shape), gradient.reshape((3,) + shape))


def lap_eigen(wave, length):
    return 2.0 * jnp.cos(2.0 * math.pi / length * wave) - 2.0


def hartley(length):
    indices = np.arange(length)
    angles = 2.0 * np.pi / length * (indices[:, None] * indices[None, :] % length)
    return jnp.asarray((np.cos(angles) + np.sin(angles)).astype(np.float32))


def matmul(a, b):
    return jnp.matmul(a, b, precision=lax.Precision.HIGHEST)


def exchange(packed, axis):
    return lax.all_to_all(packed, axis, split_axis=0, concat_axis=0, tiled=True)


def solve_potential(density, my_row, my_column, rows_count, cols_count):
    block_x, block_y, _ = density.shape
    rows_y = GY // rows_count
    cols_z = GZ // cols_count
    table_x, table_y, table_z = hartley(GX), hartley(GY), hartley(GZ)
    along = matmul(density.reshape(block_x * block_y, GZ), table_z)
    packed = along.reshape(block_x, block_y, cols_count, cols_z).transpose(2, 1, 3, 0)
    mid = exchange(packed.reshape(GY, cols_z * block_x), "col")
    spectrum = exchange(matmul(table_y, mid), "row")
    spectrum = (
        spectrum.reshape(rows_count, rows_y, cols_z, block_x)
        .transpose(1, 2, 0, 3)
        .reshape(rows_y * cols_z, GX)
    )
    spectrum = matmul(spectrum, table_x)
    index_x = jnp.arange(GX, dtype=jnp.int32)
    index_y = my_row * rows_y + jnp.arange(rows_y, dtype=jnp.int32)
    index_z = my_column * cols_z + jnp.arange(cols_z, dtype=jnp.int32)
    eigen = (
        lap_eigen(index_x.astype(jnp.float32), GX)[None, None, :]
        + lap_eigen(index_y.astype(jnp.float32), GY)[:, None, None]
        + lap_eigen(index_z.astype(jnp.float32), GZ)[None, :, None]
    )
    zero_mode = (
        (index_x == 0)[None, None, :]
        & (index_y == 0)[:, None, None]
        & (index_z == 0)[None, :, None]
    )
    scale = 1.0 / (GX * GY * GZ)
    green = jnp.where(
        zero_mode, 0.0, four_pi_g * scale / jnp.where(zero_mode, -1.0, eigen)
    ).reshape(rows_y * cols_z, GX)
    back = matmul(spectrum * green, table_x)
    packed = back.reshape(rows_y, cols_z, rows_count, block_x).transpose(2, 0, 1, 3)
    mid = exchange(packed.reshape(GY, cols_z * block_x), "row")
    returned = exchange(matmul(table_y, mid), "col")
    returned = (
        returned.reshape(cols_count, block_y, cols_z, block_x)
        .transpose(3, 1, 0, 2)
        .reshape(block_x * block_y, GZ)
    )
    return matmul(returned, table_z).reshape(block_x, block_y, GZ)


def potential_gradient(potential):
    low_x, high_x = edges(potential, "row", 0, 1)
    low_y, high_y = edges(potential, "col", 1, 1)
    wide_x = jnp.concatenate([low_x, potential, high_x], axis=0)
    wide_y = jnp.concatenate([low_y, potential, high_y], axis=1)
    return jnp.stack(
        [
            0.5 * (wide_x[2:] - wide_x[:-2]),
            0.5 * (wide_y[:, 2:] - wide_y[:, :-2]),
            0.5 * (jnp.roll(potential, -1, 2) - jnp.roll(potential, 1, 2)),
        ]
    )


def on_device(fields, counts):
    rows_count = lax.axis_size("row")
    cols_count = lax.axis_size("col")
    my_row = lax.axis_index("row")
    my_column = lax.axis_index("col")
    capacity = fields.shape[0]
    block_x = GX // rows_count
    block_y = GY // cols_count
    lat_x = block_x // PE
    lat_y = GY // PE
    lat_z = GZ // PE
    brick_y = min(PE, block_y)
    per_pencil_y = block_y // brick_y
    repeat_y = max(1, block_y // PE)
    per_peer = capacity // lat_y * repeat_y
    rows = 5 * PE * (brick_y // SUB)
    buffer_rows = cols_count * per_peer
    row_counts = lax.all_gather(counts, "col", axis=1, tiled=True).reshape(cols_count)
    starts = jnp.cumsum(row_counts) - row_counts
    column_ids = jnp.arange(cols_count, dtype=jnp.int32)
    own_start = jnp.sum(jnp.where(column_ids == my_column, starts, 0)).astype(jnp.int32)
    own_count = counts[0, 0]
    grid_xl = jnp.arange(lat_x, dtype=jnp.int32)[:, None, None]
    grid_w = jnp.arange(per_pencil_y, dtype=jnp.int32)[None, :, None]
    grid_zl = jnp.arange(lat_z, dtype=jnp.int32)[None, None, :]
    pencil_y = (my_column * block_y + grid_w * brick_y) // PE
    curve_pos = (grid_xl * lat_z + grid_zl) * lat_y + pencil_y
    curve_pos = curve_pos.reshape(-1)
    y_flat = jnp.broadcast_to(pencil_y, (lat_x, per_pencil_y, lat_z)).reshape(-1)
    owner = jnp.sum((starts[None, :] <= curve_pos[:, None]).astype(jnp.int32), axis=1) - 1
    owner_start = jnp.sum(
        jnp.where(column_ids[None, :] == owner[:, None], starts[None, :], 0), axis=1
    )
    source_index = (
        owner * per_peer + (curve_pos - owner_start) // lat_y * repeat_y + y_flat % repeat_y
    ).astype(jnp.int32)
    send_buffer = pack_slots(
        fields, own_start, cols_count, block_y, brick_y, lat_y, repeat_y
    )
    arrived = exchange(send_buffer.reshape(buffer_rows, rows, LANES), "col")
    pencil = gather_bricks(arrived, source_index, lat_x, per_pencil_y, brick_y)
    extended = padded(pencil, (("row", 1), ("col", 2)), 4)
    stepped = advance(extended)
    potential = solve_potential(stepped[0], my_row, my_column, rows_count, cols_count)
    return_buffer = kick_bricks(
        stepped,
        potential_gradient(potential),
        source_index,
        buffer_rows,
        lat_x,
        per_pencil_y,
        brick_y,
    )
    came_back = exchange(return_buffer, "col").reshape(send_buffer.shape)
    return unpack_slots(came_back, own_start, own_count, block_y, brick_y, lat_y)


def solution(mesh):
    return jax.shard_map(
        on_device,
        mesh=mesh,
        in_specs=(P(("row", "col"), None, None), P("row", "col")),
        out_specs=P(("row", "col"), None, None),
        check_vma=False,
    )
```

```python
import functools
import math

import jax
import jax.numpy as jnp
import numpy as np
from jax import lax
from jax.experimental import pallas as pl
from jax.experimental.pallas import tpu as pltpu
from jax.sharding import PartitionSpec as P

PE = 16
GX = 256
GY = 256
GZ = 128
LANES = 128
SUB = 8
TOGETHER = 5
VMEM_BYTES = 56 * 1024 * 1024


gamma_gas = 1.4
speed_bound = 4.0
time_step = 0.03
four_pi_g = 10.0


def ring_order(axis):
    count = lax.axis_size(axis)
    if axis == "col" and count == 8:
        return [0, 2, 4, 6, 7, 5, 3, 1]
    return list(range(count))


def block_of(axis):
    order = ring_order(axis)
    return [order.index(i) for i in range(len(order))]


def shift_pair(axis):
    order = ring_order(axis)
    count = len(order)
    forward = [(order[i], order[(i + 1) % count]) for i in range(count)]
    backward = [(target, source) for source, target in forward]
    return forward, backward


def edges(block, axis, dim, width):
    forward, backward = shift_pair(axis)
    low = lax.ppermute(
        lax.slice_in_dim(block, block.shape[dim] - width, None, axis=dim), axis, forward
    )
    high = lax.ppermute(lax.slice_in_dim(block, 0, width, axis=dim), axis, backward)
    return low, high


def padded(block, sides, width):
    for axis, dim in sides:
        low, high = edges(block, axis, dim, width)
        block = jnp.concatenate([low, block, high], axis=dim)
    return block


def half_flux(state, direction):
    density, momenta, energy = state[0], state[1:4], state[4]
    inverse = 1.0 / density
    velocity = momenta[direction] * inverse
    kinetic = (
        0.5
        * (momenta[0] * momenta[0] + momenta[1] * momenta[1] + momenta[2] * momenta[2])
        * inverse
    )
    pressure = (gamma_gas - 1.0) * (energy - kinetic)
    half_velocity = 0.5 * velocity
    pieces = [0.5 * momenta[direction]]
    for component in range(3):
        term = momenta[component] * half_velocity
        if component == direction:
            term = term + 0.5 * pressure
        pieces.append(term)
    pieces.append((energy + pressure) * half_velocity)
    return pieces


def side_terms(lower_gap, centre, upper_gap, direction):
    left, right = [], []
    for low, mid, high in zip(lower_gap, centre, upper_gap):
        slope = jnp.maximum(jnp.minimum(low, high), 0.0) + jnp.minimum(
            jnp.maximum(low, high), 0.0
        )
        left.append(mid + 0.5 * slope)
        right.append(mid - 0.5 * slope)
    damping = 0.5 * speed_bound
    below = [f + damping * u for f, u in zip(half_flux(left, direction), left)]
    above = [f - damping * u for f, u in zip(half_flux(right, direction), right)]
    return below, above


def step_kernel(ext_ref, out_ref, first_ref, part_ref, last_ref):
    planes = ext_ref.shape[1]
    depth_y = ext_ref.shape[2]
    out_y = out_ref.shape[2]

    def plane(ref, i):
        return [ref[q, i] for q in range(5)]

    def x_terms(ref, i):
        low, mid, high = plane(ref, i - 1), plane(ref, i), plane(ref, i + 1)
        return side_terms(
            [m - l for l, m in zip(low, mid)], mid, [h - m for m, h in zip(mid, high)], 0
        )

    def begin(ref, i):
        before, _ = x_terms(ref, i - 1)
        below, above = x_terms(ref, i)
        for q in range(5):
            last_ref[q] = below[q]
            part_ref[q] = below[q] - above[q] - before[q]

    def change(ref, i):
        below, above = x_terms(ref, i + 1)
        total = []
        for q in range(5):
            total.append(part_ref[q] + above[q])
            part_ref[q] = below[q] - above[q] - last_ref[q]
            last_ref[q] = below[q]
        mid = plane(ref, i)
        for direction, axis, size in ((1, 0, depth_y), (2, 1, LANES)):
            upper_gap = [pltpu.roll(m, size - 1, axis) - m for m in mid]
            lower_gap = [pltpu.roll(g, 1, axis) for g in upper_gap]
            below, above = side_terms(lower_gap, mid, upper_gap, direction)
            total = [
                t + (b - a) + (pltpu.roll(a, size - 1, axis) - pltpu.roll(b, 1, axis))
                for t, b, a in zip(total, below, above)
            ]
        return mid, total

    begin(ext_ref, 2)

    def first_step(i, carry):
        mid, total = change(ext_ref, i)
        for q in range(5):
            first_ref[q, i] = mid[q] - time_step * total[q]
        return carry

    lax.fori_loop(2, planes - 2, first_step, 0)
    begin(first_ref, 4)

    def second_step(i, carry):
        mid, total = change(first_ref, i)
        for q in range(5):
            value = 0.5 * ext_ref[q, i] + 0.5 * (mid[q] - time_step * total[q])
            out_ref[q, i - 4] = pltpu.roll(value, depth_y - 4, 0)[:out_y]
        return carry

    lax.fori_loop(4, planes - 4, second_step, 0)


def advance(extended):
    _, planes, depth_y, depth_z = extended.shape
    out_shape = (5, planes - 8, depth_y - 8, depth_z)
    cells = planes * depth_y * depth_z
    return pl.pallas_call(
        step_kernel,
        out_shape=jax.ShapeDtypeStruct(out_shape, jnp.float32),
        in_specs=[pl.BlockSpec(memory_space=pltpu.VMEM)],
        out_specs=pl.BlockSpec(memory_space=pltpu.VMEM),
        scratch_shapes=[
            pltpu.VMEM((5, planes, depth_y, depth_z), jnp.float32),
            pltpu.VMEM((5, depth_y, depth_z), jnp.float32),
            pltpu.VMEM((5, depth_y, depth_z), jnp.float32),
        ],
        compiler_params=pltpu.CompilerParams(vmem_limit_bytes=VMEM_BYTES),
        cost_estimate=pl.CostEstimate(
            flops=900 * cells, bytes_accessed=40 * cells, transcendentals=0
        ),
        name="gas_step",
    )(extended)


def pack_kernel(start_ref, in_ref, out_ref, rows_ref):
    cols_count, _, repeat_y, rows, _ = out_ref.shape
    lat_y = in_ref.shape[1]
    bricks = cols_count * repeat_y
    per_patch = bricks // lat_y
    halves = 2 // per_patch
    offset = lax.rem(start_ref[0], lat_y)

    for q in range(5):

        def chunk(a, carry):
            for brick in range(per_patch):
                for half in range(halves):
                    lane = pl.multiple_of((2 * a + brick * halves + half) * LANES, LANES)
                    value = pltpu.roll(in_ref[q, :, pl.ds(lane, LANES)], offset, 0)
                    row = brick * rows + (q * PE + a) * halves + half
                    for part in range(lat_y // SUB):
                        rows_ref[
                            pl.ds(
                                part * SUB * per_patch * rows + row,
                                SUB,
                                stride=per_patch * rows,
                            ),
                            :,
                        ] = value[part * SUB : (part + 1) * SUB]
            return carry

        lax.fori_loop(0, PE, chunk, 0, unroll=4)

    for i, block in enumerate(block_of("col")):
        for inner in range(repeat_y):
            out_ref[i, 0, inner] = rows_ref[pl.ds((block * repeat_y + inner) * rows, rows), :]


def pack_slots(fields, own_start, cols_count, brick_y, lat_y, repeat_y):
    capacity = fields.shape[0]
    groups = capacity // lat_y
    rows = 5 * PE * (brick_y // SUB)
    return pl.pallas_call(
        pack_kernel,
        out_shape=jax.ShapeDtypeStruct(
            (cols_count, groups, repeat_y, rows, LANES), jnp.float32
        ),
        grid_spec=pltpu.PrefetchScalarGridSpec(
            num_scalar_prefetch=1,
            grid=(groups,),
            in_specs=[pl.BlockSpec((5, lat_y, PE * PE * PE), lambda g, s: (0, g, 0))],
            out_specs=pl.BlockSpec(
                (cols_count, 1, repeat_y, rows, LANES), lambda g, s: (0, g, 0, 0, 0)
            ),
            scratch_shapes=[pltpu.VMEM((cols_count * repeat_y * rows, LANES), jnp.float32)],
        ),
        compiler_params=pltpu.CompilerParams(vmem_limit_bytes=VMEM_BYTES),
        name="pack_slots",
    )(own_start.reshape(1), fields.transpose(1, 0, 2))


def unpack_kernel(info_ref, in_ref, out_ref, rows_ref):
    cols_count, _, repeat_y, rows, _ = in_ref.shape
    lat_y = out_ref.shape[1]
    bricks = cols_count * repeat_y
    per_patch = bricks // lat_y
    halves = 2 // per_patch
    offset = lax.rem(lat_y - lax.rem(info_ref[0], lat_y), lat_y)
    for i, block in enumerate(block_of("col")):
        for inner in range(repeat_y):
            rows_ref[pl.ds((block * repeat_y + inner) * rows, rows), :] = in_ref[i, 0, inner]
    slot = pl.program_id(0) * lat_y + lax.broadcasted_iota(jnp.int32, (lat_y, LANES), 0)
    live = slot < info_ref[1]

    for q in range(5):

        def chunk(a, carry):
            for brick in range(per_patch):
                for half in range(halves):
                    lane = pl.multiple_of((2 * a + brick * halves + half) * LANES, LANES)
                    row = brick * rows + (q * PE + a) * halves + half
                    value = jnp.concatenate(
                        [
                            rows_ref[
                                pl.ds(
                                    part * SUB * per_patch * rows + row,
                                    SUB,
                                    stride=per_patch * rows,
                                ),
                                :,
                            ]
                            for part in range(lat_y // SUB)
                        ],
                        axis=0,
                    )
                    value = pltpu.roll(value, offset, 0)
                    out_ref[q, :, pl.ds(lane, LANES)] = jnp.where(live, value, 0.0)
            return carry

        lax.fori_loop(0, PE, chunk, 0, unroll=4)


def unpack_slots(arrived, own_start, own_count, lat_y):
    cols_count, groups, repeat_y, rows, _ = arrived.shape
    out = pl.pallas_call(
        unpack_kernel,
        out_shape=jax.ShapeDtypeStruct((5, groups * lat_y, PE * PE * PE), jnp.float32),
        grid_spec=pltpu.PrefetchScalarGridSpec(
            num_scalar_prefetch=1,
            grid=(groups,),
            in_specs=[
                pl.BlockSpec(
                    (cols_count, 1, repeat_y, rows, LANES), lambda g, s: (0, g, 0, 0, 0)
                )
            ],
            out_specs=pl.BlockSpec((5, lat_y, PE * PE * PE), lambda g, s: (0, g, 0)),
            scratch_shapes=[pltpu.VMEM((cols_count * repeat_y * rows, LANES), jnp.float32)],
        ),
        compiler_params=pltpu.CompilerParams(vmem_limit_bytes=VMEM_BYTES),
        name="unpack_slots",
    )(jnp.stack([own_start, own_count]), arrived)
    return out.transpose(1, 0, 2)


def swap_many(many):
    lane = lax.broadcasted_iota(jnp.int32, (SUB, LANES), 1)
    step = 1
    while step < GZ // PE:
        shift = step * PE
        low = (lane // shift) % 2 == 0
        result = []
        for values in many:
            swapped = list(values)
            for i, one in enumerate(values):
                if i & step == 0:
                    two = values[i | step]
                    swapped[i] = jnp.where(low, one, pltpu.roll(two, shift, 1))
                    swapped[i | step] = jnp.where(low, pltpu.roll(one, LANES - shift, 1), two)
            result.append(swapped)
        many = result
        step *= 2
    return many


def gather_kernel(index_ref, *refs):
    lat_z = GZ // PE
    in_refs, out_ref, rows_ref = refs[:lat_z], refs[lat_z], refs[lat_z + 1]
    brick_y = out_ref.shape[3]
    groups = in_refs[0].shape[1] // SUB

    def regroup(n, carry):
        firsts = [n * TOGETHER + m for m in range(TOGETHER)]
        values = [
            [ref[0, pl.ds(pl.multiple_of(m * SUB, SUB), SUB), :] for ref in in_refs]
            for m in firsts
        ]
        for m, swapped in zip(firsts, swap_many(values)):
            for b in range(SUB):
                rows_ref[pl.ds(m * (SUB * SUB) + b, SUB, stride=SUB), :] = swapped[b]
        return carry

    lax.fori_loop(0, groups // TOGETHER, regroup, 0)
    for q in range(5):
        for a in range(PE):
            out_ref[q, a, 0] = rows_ref[pl.ds((q * PE + a) * brick_y, brick_y), :]


def gather_bricks(arrived, source_index, lat_x, per_pencil_y, brick_y):
    lat_z = GZ // PE
    rows = arrived.shape[1]

    def picked(zl):
        return lambda i, w, index: (index[(i * per_pencil_y + w) * lat_z + zl], 0, 0)

    out = pl.pallas_call(
        gather_kernel,
        out_shape=jax.ShapeDtypeStruct(
            (5, lat_x * PE, per_pencil_y, brick_y, LANES), jnp.float32
        ),
        grid_spec=pltpu.PrefetchScalarGridSpec(
            num_scalar_prefetch=1,
            grid=(lat_x, per_pencil_y),
            in_specs=[pl.BlockSpec((1, rows, LANES), picked(zl)) for zl in range(lat_z)],
            out_specs=pl.BlockSpec(
                (5, PE, 1, brick_y, LANES), lambda i, w, index: (0, i, w, 0, 0)
            ),
            scratch_shapes=[pltpu.VMEM((rows * SUB, LANES), jnp.float32)],
        ),
        compiler_params=pltpu.CompilerParams(vmem_limit_bytes=VMEM_BYTES),
        name="gather_bricks",
    )(source_index, *([arrived] * lat_z))
    return out.reshape(5, lat_x * PE, per_pencil_y * brick_y, GZ)


def kick_kernel(index_ref, state_ref, gradient_ref, out_ref, rows_ref, brick_ref, sems):
    lat_z = GZ // PE
    brick_y = state_ref.shape[3]
    groups = brick_ref.shape[1] // SUB
    at_grid = (pl.program_id(0) * pl.num_programs(1) + pl.program_id(1)) * lat_z

    def kick(a, carry):
        density = state_ref[0, a, 0]
        momenta = [state_ref[1 + d, a, 0] for d in range(3)]
        slopes = [gradient_ref[d, a, 0] for d in range(3)]
        work = momenta[0] * slopes[0] + momenta[1] * slopes[1] + momenta[2] * slopes[2]
        pieces = [density]
        for d in range(3):
            pieces.append(momenta[d] - time_step * density * slopes[d])
        pieces.append(state_ref[4, a, 0] - time_step * work)
        for q in range(5):
            at = pl.multiple_of((q * PE + a) * brick_y, SUB)
            rows_ref[pl.ds(at, brick_y), :] = pieces[q]
        return carry

    lax.fori_loop(0, PE, kick, 0, unroll=4)

    def regroup(n, carry):
        firsts = [n * TOGETHER + m for m in range(TOGETHER)]
        values = [
            [rows_ref[pl.ds(m * (SUB * SUB) + b, SUB, stride=SUB), :] for b in range(SUB)]
            for m in firsts
        ]
        for m, swapped in zip(firsts, swap_many(values)):
            for zl in range(lat_z):
                brick_ref[zl, pl.ds(pl.multiple_of(m * SUB, SUB), SUB), :] = swapped[zl]
        return carry

    lax.fori_loop(0, groups // TOGETHER, regroup, 0)
    copies = [
        pltpu.make_async_copy(
            brick_ref.at[zl], out_ref.at[index_ref[at_grid + zl]], sems.at[zl]
        )
        for zl in range(lat_z)
    ]
    for copy in copies:
        copy.start()
    for copy in copies:
        copy.wait()


def kick_bricks(stepped, gradient, source_index, buffer_rows, lat_x, per_pencil_y, brick_y):
    lat_z = GZ // PE
    rows = 5 * PE * (brick_y // SUB)
    shape = (lat_x * PE, per_pencil_y, brick_y, GZ)

    def block(count):
        return pl.BlockSpec((count, PE, 1, brick_y, GZ), lambda i, w, index: (0, i, w, 0, 0))

    return pl.pallas_call(
        kick_kernel,
        out_shape=jax.ShapeDtypeStruct((buffer_rows, rows, LANES), jnp.float32),
        grid_spec=pltpu.PrefetchScalarGridSpec(
            num_scalar_prefetch=1,
            grid=(lat_x, per_pencil_y),
            in_specs=[block(5), block(3)],
            out_specs=pl.BlockSpec(memory_space=pl.ANY),
            scratch_shapes=[
                pltpu.VMEM((rows * SUB, LANES), jnp.float32),
                pltpu.VMEM((lat_z, rows, LANES), jnp.float32),
                pltpu.SemaphoreType.DMA((lat_z,)),
            ],
        ),
        compiler_params=pltpu.CompilerParams(vmem_limit_bytes=VMEM_BYTES),
        name="kick_bricks",
    )(source_index, stepped.reshape((5,) + shape), gradient.reshape((3,) + shape))


def lap_eigen(wave, length):
    return 2.0 * jnp.cos(2.0 * math.pi / length * wave) - 2.0


def hartley(length):
    indices = np.arange(length)
    angles = 2.0 * np.pi / length * (indices[:, None] * indices[None, :] % length)
    return jnp.asarray((np.cos(angles) + np.sin(angles)).astype(np.float32))


def matmul(a, b):
    return jnp.matmul(a, b, precision=lax.Precision.HIGHEST)


def exchange(packed, axis):
    return lax.all_to_all(packed, axis, split_axis=0, concat_axis=0, tiled=True)


def solve_potential(density, my_row, my_column, rows_count, cols_count):
    block_x, block_y, _ = density.shape
    rows_y = GY // rows_count
    cols_z = GZ // cols_count
    table_x, table_y, table_z = hartley(GX), hartley(GY), hartley(GZ)
    table_y = jnp.concatenate(
        [table_y[block * block_y : (block + 1) * block_y] for block in block_of("col")]
    )
    along = matmul(density.reshape(block_x * block_y, GZ), table_z)
    packed = along.reshape(block_x, block_y, cols_count, cols_z).transpose(2, 1, 3, 0)
    mid = exchange(packed.reshape(GY, cols_z * block_x), "col")
    spectrum = exchange(matmul(table_y.T, mid), "row")
    spectrum = (
        spectrum.reshape(rows_count, rows_y, cols_z, block_x)
        .transpose(1, 2, 0, 3)
        .reshape(rows_y * cols_z, GX)
    )
    spectrum = matmul(spectrum, table_x)
    index_x = jnp.arange(GX, dtype=jnp.int32)
    index_y = my_row * rows_y + jnp.arange(rows_y, dtype=jnp.int32)
    index_z = my_column * cols_z + jnp.arange(cols_z, dtype=jnp.int32)
    eigen = (
        lap_eigen(index_x.astype(jnp.float32), GX)[None, None, :]
        + lap_eigen(index_y.astype(jnp.float32), GY)[:, None, None]
        + lap_eigen(index_z.astype(jnp.float32), GZ)[None, :, None]
    )
    zero_mode = (
        (index_x == 0)[None, None, :]
        & (index_y == 0)[:, None, None]
        & (index_z == 0)[None, :, None]
    )
    scale = 1.0 / (GX * GY * GZ)
    green = jnp.where(
        zero_mode, 0.0, four_pi_g * scale / jnp.where(zero_mode, -1.0, eigen)
    ).reshape(rows_y * cols_z, GX)
    back = matmul(spectrum * green, table_x)
    packed = back.reshape(rows_y, cols_z, rows_count, block_x).transpose(2, 0, 1, 3)
    mid = exchange(packed.reshape(GY, cols_z * block_x), "row")
    returned = exchange(matmul(table_y, mid), "col")
    returned = (
        returned.reshape(cols_count, block_y, cols_z, block_x)
        .transpose(3, 1, 0, 2)
        .reshape(block_x * block_y, GZ)
    )
    return matmul(returned, table_z).reshape(block_x, block_y, GZ)


def potential_gradient(potential):
    low_x, high_x = edges(potential, "row", 0, 1)
    low_y, high_y = edges(potential, "col", 1, 1)
    wide_x = jnp.concatenate([low_x, potential, high_x], axis=0)
    wide_y = jnp.concatenate([low_y, potential, high_y], axis=1)
    return jnp.stack(
        [
            0.5 * (wide_x[2:] - wide_x[:-2]),
            0.5 * (wide_y[:, 2:] - wide_y[:, :-2]),
            0.5 * (jnp.roll(potential, -1, 2) - jnp.roll(potential, 1, 2)),
        ]
    )


def on_device(fields, counts):
    rows_count = lax.axis_size("row")
    cols_count = lax.axis_size("col")
    my_row = lax.axis_index("row")
    my_column = lax.axis_index("col")
    capacity = fields.shape[0]
    block_x = GX // rows_count
    block_y = GY // cols_count
    lat_x = block_x // PE
    lat_y = GY // PE
    lat_z = GZ // PE
    brick_y = min(PE, block_y)
    per_pencil_y = block_y // brick_y
    repeat_y = max(1, block_y // PE)
    per_peer = capacity // lat_y * repeat_y
    rows = 5 * PE * (brick_y // SUB)
    buffer_rows = cols_count * per_peer
    row_counts = lax.all_gather(counts, "col", axis=1, tiled=True).reshape(cols_count)
    starts = jnp.cumsum(row_counts) - row_counts
    column_ids = jnp.arange(cols_count, dtype=jnp.int32)
    own_start = jnp.sum(jnp.where(column_ids == my_column, starts, 0)).astype(jnp.int32)
    own_count = counts[0, 0]
    block_ids = jnp.array(block_of("col"), jnp.int32)
    my_block = jnp.sum(jnp.where(column_ids == my_column, block_ids, 0)).astype(jnp.int32)
    grid_xl = jnp.arange(lat_x, dtype=jnp.int32)[:, None, None]
    grid_w = jnp.arange(per_pencil_y, dtype=jnp.int32)[None, :, None]
    grid_zl = jnp.arange(lat_z, dtype=jnp.int32)[None, None, :]
    pencil_y = (my_block * block_y + grid_w * brick_y) // PE
    curve_pos = (grid_xl * lat_z + grid_zl) * lat_y + pencil_y
    curve_pos = curve_pos.reshape(-1)
    y_flat = jnp.broadcast_to(pencil_y, (lat_x, per_pencil_y, lat_z)).reshape(-1)
    owner = jnp.sum((starts[None, :] <= curve_pos[:, None]).astype(jnp.int32), axis=1) - 1
    owner_start = jnp.sum(
        jnp.where(column_ids[None, :] == owner[:, None], starts[None, :], 0), axis=1
    )
    source_index = (
        owner * per_peer + (curve_pos - owner_start) // lat_y * repeat_y + y_flat % repeat_y
    ).astype(jnp.int32)
    send_buffer = pack_slots(fields, own_start, cols_count, brick_y, lat_y, repeat_y)
    arrived = exchange(send_buffer.reshape(buffer_rows, rows, LANES), "col")
    pencil = gather_bricks(arrived, source_index, lat_x, per_pencil_y, brick_y)
    extended = padded(pencil, (("row", 1), ("col", 2)), 4)
    stepped = advance(extended)
    potential = solve_potential(stepped[0], my_row, my_column, rows_count, cols_count)
    return_buffer = kick_bricks(
        stepped,
        potential_gradient(potential),
        source_index,
        buffer_rows,
        lat_x,
        per_pencil_y,
        brick_y,
    )
    came_back = exchange(return_buffer, "col").reshape(send_buffer.shape)
    return unpack_slots(came_back, own_start, own_count, lat_y)


def solution(mesh):
    return jax.shard_map(
        on_device,
        mesh=mesh,
        in_specs=(P(("row", "col"), None, None), P("row", "col")),
        out_specs=P(("row", "col"), None, None),
        check_vma=False,
    )
```

```python
import functools
import math

import jax
import jax.numpy as jnp
import numpy as np
from jax import lax
from jax.experimental import pallas as pl
from jax.experimental.pallas import tpu as pltpu
from jax.sharding import PartitionSpec as P

PE = 16
GX = 256
GY = 256
GZ = 128
LANES = 128
SUB = 8
TOGETHER = 5
VMEM_BYTES = 56 * 1024 * 1024


gamma_gas = 1.4
speed_bound = 4.0
time_step = 0.03
four_pi_g = 10.0


def ring_order(axis):
    count = lax.axis_size(axis)
    if axis == "col" and count == 8:
        return [0, 2, 4, 6, 7, 5, 3, 1]
    return list(range(count))


def block_of(axis):
    order = ring_order(axis)
    return [order.index(i) for i in range(len(order))]


def shift_pair(axis):
    order = ring_order(axis)
    count = len(order)
    forward = [(order[i], order[(i + 1) % count]) for i in range(count)]
    backward = [(target, source) for source, target in forward]
    return forward, backward


def edges(block, axis, dim, width):
    forward, backward = shift_pair(axis)
    low = lax.ppermute(
        lax.slice_in_dim(block, block.shape[dim] - width, None, axis=dim), axis, forward
    )
    high = lax.ppermute(lax.slice_in_dim(block, 0, width, axis=dim), axis, backward)
    return low, high


def padded(block, sides, width):
    for axis, dim in sides:
        low, high = edges(block, axis, dim, width)
        block = jnp.concatenate([low, block, high], axis=dim)
    return block


def half_flux(state, direction):
    density, momenta, energy = state[0], state[1:4], state[4]
    inverse = 1.0 / density
    velocity = momenta[direction] * inverse
    kinetic = (
        0.5
        * (momenta[0] * momenta[0] + momenta[1] * momenta[1] + momenta[2] * momenta[2])
        * inverse
    )
    pressure = (gamma_gas - 1.0) * (energy - kinetic)
    half_velocity = 0.5 * velocity
    pieces = [0.5 * momenta[direction]]
    for component in range(3):
        term = momenta[component] * half_velocity
        if component == direction:
            term = term + 0.5 * pressure
        pieces.append(term)
    pieces.append((energy + pressure) * half_velocity)
    return pieces


def side_terms(lower_gap, centre, upper_gap, direction):
    left, right = [], []
    for low, mid, high in zip(lower_gap, centre, upper_gap):
        slope = jnp.maximum(jnp.minimum(low, high), 0.0) + jnp.minimum(
            jnp.maximum(low, high), 0.0
        )
        left.append(mid + 0.5 * slope)
        right.append(mid - 0.5 * slope)
    damping = 0.5 * speed_bound
    below = [f + damping * u for f, u in zip(half_flux(left, direction), left)]
    above = [f - damping * u for f, u in zip(half_flux(right, direction), right)]
    return below, above


def step_kernel(ext_ref, out_ref, first_ref, part_ref, last_ref):
    planes = ext_ref.shape[1]
    depth_y = ext_ref.shape[2]
    out_y = out_ref.shape[2]

    def plane(ref, i):
        return [ref[q, i] for q in range(5)]

    def x_terms(ref, i):
        low, mid, high = plane(ref, i - 1), plane(ref, i), plane(ref, i + 1)
        return side_terms(
            [m - l for l, m in zip(low, mid)], mid, [h - m for m, h in zip(mid, high)], 0
        )

    def begin(ref, i):
        before, _ = x_terms(ref, i - 1)
        below, above = x_terms(ref, i)
        for q in range(5):
            last_ref[q] = below[q]
            part_ref[q] = below[q] - above[q] - before[q]

    def change(ref, i):
        below, above = x_terms(ref, i + 1)
        total = []
        for q in range(5):
            total.append(part_ref[q] + above[q])
            part_ref[q] = below[q] - above[q] - last_ref[q]
            last_ref[q] = below[q]
        mid = plane(ref, i)
        for direction, axis, size in ((1, 0, depth_y), (2, 1, LANES)):
            upper_gap = [pltpu.roll(m, size - 1, axis) - m for m in mid]
            lower_gap = [pltpu.roll(g, 1, axis) for g in upper_gap]
            below, above = side_terms(lower_gap, mid, upper_gap, direction)
            total = [
                t + (b - a) + (pltpu.roll(a, size - 1, axis) - pltpu.roll(b, 1, axis))
                for t, b, a in zip(total, below, above)
            ]
        return mid, total

    begin(ext_ref, 2)

    def first_step(i, carry):
        mid, total = change(ext_ref, i)
        for q in range(5):
            first_ref[q, i] = mid[q] - time_step * total[q]
        return carry

    lax.fori_loop(2, planes - 2, first_step, 0)
    begin(first_ref, 4)

    def second_step(i, carry):
        mid, total = change(first_ref, i)
        for q in range(5):
            value = 0.5 * ext_ref[q, i] + 0.5 * (mid[q] - time_step * total[q])
            out_ref[q, i - 4] = pltpu.roll(value, depth_y - 4, 0)[:out_y]
        return carry

    lax.fori_loop(4, planes - 4, second_step, 0)


def advance(extended):
    _, planes, depth_y, depth_z = extended.shape
    out_shape = (5, planes - 8, depth_y - 8, depth_z)
    cells = planes * depth_y * depth_z
    return pl.pallas_call(
        step_kernel,
        out_shape=jax.ShapeDtypeStruct(out_shape, jnp.float32),
        in_specs=[pl.BlockSpec(memory_space=pltpu.VMEM)],
        out_specs=pl.BlockSpec(memory_space=pltpu.VMEM),
        scratch_shapes=[
            pltpu.VMEM((5, planes, depth_y, depth_z), jnp.float32),
            pltpu.VMEM((5, depth_y, depth_z), jnp.float32),
            pltpu.VMEM((5, depth_y, depth_z), jnp.float32),
        ],
        compiler_params=pltpu.CompilerParams(vmem_limit_bytes=VMEM_BYTES),
        cost_estimate=pl.CostEstimate(
            flops=900 * cells, bytes_accessed=40 * cells, transcendentals=0
        ),
        name="gas_step",
    )(extended)


def pack_kernel(start_ref, in_ref, out_ref, rows_ref):
    cols_count, _, repeat_y, rows, _ = out_ref.shape
    lat_y = in_ref.shape[1]
    bricks = cols_count * repeat_y
    per_patch = bricks // lat_y
    halves = 2 // per_patch
    offset = lax.rem(start_ref[0], lat_y)

    for q in range(5):

        def chunk(a, carry):
            for brick in range(per_patch):
                for half in range(halves):
                    lane = pl.multiple_of((2 * a + brick * halves + half) * LANES, LANES)
                    value = pltpu.roll(in_ref[q, :, pl.ds(lane, LANES)], offset, 0)
                    row = brick * rows + (q * PE + a) * halves + half
                    for part in range(lat_y // SUB):
                        rows_ref[
                            pl.ds(
                                part * SUB * per_patch * rows + row,
                                SUB,
                                stride=per_patch * rows,
                            ),
                            :,
                        ] = value[part * SUB : (part + 1) * SUB]
            return carry

        lax.fori_loop(0, PE, chunk, 0, unroll=4)

    for i, block in enumerate(block_of("col")):
        for inner in range(repeat_y):
            out_ref[i, 0, inner] = rows_ref[pl.ds((block * repeat_y + inner) * rows, rows), :]


def pack_slots(fields, own_start, cols_count, brick_y, lat_y, repeat_y):
    capacity = fields.shape[0]
    groups = capacity // lat_y
    rows = 5 * PE * (brick_y // SUB)
    return pl.pallas_call(
        pack_kernel,
        out_shape=jax.ShapeDtypeStruct(
            (cols_count, groups, repeat_y, rows, LANES), jnp.float32
        ),
        grid_spec=pltpu.PrefetchScalarGridSpec(
            num_scalar_prefetch=1,
            grid=(groups,),
            in_specs=[pl.BlockSpec((5, lat_y, PE * PE * PE), lambda g, s: (0, g, 0))],
            out_specs=pl.BlockSpec(
                (cols_count, 1, repeat_y, rows, LANES), lambda g, s: (0, g, 0, 0, 0)
            ),
            scratch_shapes=[pltpu.VMEM((cols_count * repeat_y * rows, LANES), jnp.float32)],
        ),
        compiler_params=pltpu.CompilerParams(vmem_limit_bytes=VMEM_BYTES),
        name="pack_slots",
    )(own_start.reshape(1), fields.transpose(1, 0, 2))


def unpack_kernel(info_ref, in_ref, out_ref, rows_ref):
    cols_count, _, repeat_y, rows, _ = in_ref.shape
    lat_y = out_ref.shape[1]
    bricks = cols_count * repeat_y
    per_patch = bricks // lat_y
    halves = 2 // per_patch
    offset = lax.rem(lat_y - lax.rem(info_ref[0], lat_y), lat_y)
    for i, block in enumerate(block_of("col")):
        for inner in range(repeat_y):
            rows_ref[pl.ds((block * repeat_y + inner) * rows, rows), :] = in_ref[i, 0, inner]
    slot = pl.program_id(0) * lat_y + lax.broadcasted_iota(jnp.int32, (lat_y, LANES), 0)
    live = slot < info_ref[1]

    for q in range(5):

        def chunk(a, carry):
            for brick in range(per_patch):
                for half in range(halves):
                    lane = pl.multiple_of((2 * a + brick * halves + half) * LANES, LANES)
                    row = brick * rows + (q * PE + a) * halves + half
                    value = jnp.concatenate(
                        [
                            rows_ref[
                                pl.ds(
                                    part * SUB * per_patch * rows + row,
                                    SUB,
                                    stride=per_patch * rows,
                                ),
                                :,
                            ]
                            for part in range(lat_y // SUB)
                        ],
                        axis=0,
                    )
                    value = pltpu.roll(value, offset, 0)
                    out_ref[q, :, pl.ds(lane, LANES)] = jnp.where(live, value, 0.0)
            return carry

        lax.fori_loop(0, PE, chunk, 0, unroll=4)


def unpack_slots(arrived, own_start, own_count, lat_y):
    cols_count, groups, repeat_y, rows, _ = arrived.shape
    out = pl.pallas_call(
        unpack_kernel,
        out_shape=jax.ShapeDtypeStruct((5, groups * lat_y, PE * PE * PE), jnp.float32),
        grid_spec=pltpu.PrefetchScalarGridSpec(
            num_scalar_prefetch=1,
            grid=(groups,),
            in_specs=[
                pl.BlockSpec(
                    (cols_count, 1, repeat_y, rows, LANES), lambda g, s: (0, g, 0, 0, 0)
                )
            ],
            out_specs=pl.BlockSpec((5, lat_y, PE * PE * PE), lambda g, s: (0, g, 0)),
            scratch_shapes=[pltpu.VMEM((cols_count * repeat_y * rows, LANES), jnp.float32)],
        ),
        compiler_params=pltpu.CompilerParams(vmem_limit_bytes=VMEM_BYTES),
        name="unpack_slots",
    )(jnp.stack([own_start, own_count]), arrived)
    return out.transpose(1, 0, 2)


def swap_many(many):
    lane = lax.broadcasted_iota(jnp.int32, (SUB, LANES), 1)
    step = 1
    while step < GZ // PE:
        shift = step * PE
        low = (lane // shift) % 2 == 0
        result = []
        for values in many:
            swapped = list(values)
            for i, one in enumerate(values):
                if i & step == 0:
                    two = values[i | step]
                    swapped[i] = jnp.where(low, one, pltpu.roll(two, shift, 1))
                    swapped[i | step] = jnp.where(low, pltpu.roll(one, LANES - shift, 1), two)
            result.append(swapped)
        many = result
        step *= 2
    return many


def gather_kernel(index_ref, *refs):
    lat_z = GZ // PE
    in_refs, out_ref, rows_ref = refs[:lat_z], refs[lat_z], refs[lat_z + 1]
    brick_y = out_ref.shape[3]
    groups = in_refs[0].shape[1] // SUB

    def regroup(n, carry):
        firsts = [n * TOGETHER + m for m in range(TOGETHER)]
        values = [
            [ref[0, pl.ds(pl.multiple_of(m * SUB, SUB), SUB), :] for ref in in_refs]
            for m in firsts
        ]
        for m, swapped in zip(firsts, swap_many(values)):
            for b in range(SUB):
                rows_ref[pl.ds(m * (SUB * SUB) + b, SUB, stride=SUB), :] = swapped[b]
        return carry

    lax.fori_loop(0, groups // TOGETHER, regroup, 0)
    for q in range(5):
        for a in range(PE):
            out_ref[q, a, 0] = rows_ref[pl.ds((q * PE + a) * brick_y, brick_y), :]


def gather_bricks(arrived, source_index, lat_x, per_pencil_y, brick_y):
    lat_z = GZ // PE
    rows = arrived.shape[1]

    def picked(zl):
        return lambda i, w, index: (index[(i * per_pencil_y + w) * lat_z + zl], 0, 0)

    out = pl.pallas_call(
        gather_kernel,
        out_shape=jax.ShapeDtypeStruct(
            (5, lat_x * PE, per_pencil_y, brick_y, LANES), jnp.float32
        ),
        grid_spec=pltpu.PrefetchScalarGridSpec(
            num_scalar_prefetch=1,
            grid=(lat_x, per_pencil_y),
            in_specs=[pl.BlockSpec((1, rows, LANES), picked(zl)) for zl in range(lat_z)],
            out_specs=pl.BlockSpec(
                (5, PE, 1, brick_y, LANES), lambda i, w, index: (0, i, w, 0, 0)
            ),
            scratch_shapes=[pltpu.VMEM((rows * SUB, LANES), jnp.float32)],
        ),
        compiler_params=pltpu.CompilerParams(vmem_limit_bytes=VMEM_BYTES),
        name="gather_bricks",
    )(source_index, *([arrived] * lat_z))
    return out.reshape(5, lat_x * PE, per_pencil_y * brick_y, GZ)


def kick_kernel(index_ref, state_ref, gradient_ref, out_ref, rows_ref, brick_ref, sems):
    lat_z = GZ // PE
    brick_y = state_ref.shape[3]
    groups = brick_ref.shape[1] // SUB
    at_grid = (pl.program_id(0) * pl.num_programs(1) + pl.program_id(1)) * lat_z

    def kick(a, carry):
        density = state_ref[0, a, 0]
        momenta = [state_ref[1 + d, a, 0] for d in range(3)]
        slopes = [gradient_ref[d, a, 0] for d in range(3)]
        work = momenta[0] * slopes[0] + momenta[1] * slopes[1] + momenta[2] * slopes[2]
        pieces = [density]
        for d in range(3):
            pieces.append(momenta[d] - time_step * density * slopes[d])
        pieces.append(state_ref[4, a, 0] - time_step * work)
        for q in range(5):
            at = pl.multiple_of((q * PE + a) * brick_y, SUB)
            rows_ref[pl.ds(at, brick_y), :] = pieces[q]
        return carry

    lax.fori_loop(0, PE, kick, 0, unroll=4)

    def regroup(n, carry):
        firsts = [n * TOGETHER + m for m in range(TOGETHER)]
        values = [
            [rows_ref[pl.ds(m * (SUB * SUB) + b, SUB, stride=SUB), :] for b in range(SUB)]
            for m in firsts
        ]
        for m, swapped in zip(firsts, swap_many(values)):
            for zl in range(lat_z):
                brick_ref[zl, pl.ds(pl.multiple_of(m * SUB, SUB), SUB), :] = swapped[zl]
        return carry

    lax.fori_loop(0, groups // TOGETHER, regroup, 0)
    copies = [
        pltpu.make_async_copy(
            brick_ref.at[zl], out_ref.at[index_ref[at_grid + zl]], sems.at[zl]
        )
        for zl in range(lat_z)
    ]
    for copy in copies:
        copy.start()
    for copy in copies:
        copy.wait()


def kick_bricks(stepped, gradient, source_index, buffer_rows, lat_x, per_pencil_y, brick_y):
    lat_z = GZ // PE
    rows = 5 * PE * (brick_y // SUB)
    shape = (lat_x * PE, per_pencil_y, brick_y, GZ)

    def block(count):
        return pl.BlockSpec((count, PE, 1, brick_y, GZ), lambda i, w, index: (0, i, w, 0, 0))

    return pl.pallas_call(
        kick_kernel,
        out_shape=jax.ShapeDtypeStruct((buffer_rows, rows, LANES), jnp.float32),
        grid_spec=pltpu.PrefetchScalarGridSpec(
            num_scalar_prefetch=1,
            grid=(lat_x, per_pencil_y),
            in_specs=[block(5), block(3)],
            out_specs=pl.BlockSpec(memory_space=pl.ANY),
            scratch_shapes=[
                pltpu.VMEM((rows * SUB, LANES), jnp.float32),
                pltpu.VMEM((lat_z, rows, LANES), jnp.float32),
                pltpu.SemaphoreType.DMA((lat_z,)),
            ],
        ),
        compiler_params=pltpu.CompilerParams(vmem_limit_bytes=VMEM_BYTES),
        name="kick_bricks",
    )(source_index, stepped.reshape((5,) + shape), gradient.reshape((3,) + shape))


def lap_eigen(wave, length):
    return 2.0 * jnp.cos(2.0 * math.pi / length * wave) - 2.0


def hartley(length):
    indices = np.arange(length)
    angles = 2.0 * np.pi / length * (indices[:, None] * indices[None, :] % length)
    return jnp.asarray((np.cos(angles) + np.sin(angles)).astype(np.float32))


def matmul(a, b):
    return jnp.matmul(a, b, precision=lax.Precision.HIGHEST)


def exchange(packed, axis):
    return lax.all_to_all(packed, axis, split_axis=0, concat_axis=0, tiled=True)


def solve_potential(density, my_row, my_column, rows_count, cols_count):
    block_x, block_y, _ = density.shape
    rows_y = GY // rows_count
    cols_z = GZ // cols_count
    table_x, table_y, table_z = hartley(GX), hartley(GY), hartley(GZ)
    table_y = jnp.concatenate(
        [table_y[block * block_y : (block + 1) * block_y] for block in block_of("col")]
    )
    along = lax.optimization_barrier(
        matmul(density.reshape(block_x * block_y, GZ), table_z)
    )
    packed = along.reshape(block_x, block_y, cols_count, cols_z).transpose(2, 1, 3, 0)
    mid = exchange(packed.reshape(GY, cols_z * block_x), "col")
    spectrum = exchange(matmul(table_y.T, mid), "row")
    spectrum = (
        spectrum.reshape(rows_count, rows_y, cols_z, block_x)
        .transpose(1, 2, 0, 3)
        .reshape(rows_y * cols_z, GX)
    )
    spectrum = matmul(spectrum, table_x)
    index_x = jnp.arange(GX, dtype=jnp.int32)
    index_y = my_row * rows_y + jnp.arange(rows_y, dtype=jnp.int32)
    index_z = my_column * cols_z + jnp.arange(cols_z, dtype=jnp.int32)
    eigen = (
        lap_eigen(index_x.astype(jnp.float32), GX)[None, None, :]
        + lap_eigen(index_y.astype(jnp.float32), GY)[:, None, None]
        + lap_eigen(index_z.astype(jnp.float32), GZ)[None, :, None]
    )
    zero_mode = (
        (index_x == 0)[None, None, :]
        & (index_y == 0)[:, None, None]
        & (index_z == 0)[None, :, None]
    )
    scale = 1.0 / (GX * GY * GZ)
    green = jnp.where(
        zero_mode, 0.0, four_pi_g * scale / jnp.where(zero_mode, -1.0, eigen)
    ).reshape(rows_y * cols_z, GX)
    back = matmul(spectrum * green, table_x)
    packed = back.reshape(rows_y, cols_z, rows_count, block_x).transpose(2, 0, 1, 3)
    mid = exchange(packed.reshape(GY, cols_z * block_x), "row")
    returned = exchange(matmul(table_y, mid), "col")
    returned = (
        returned.reshape(cols_count, block_y, cols_z, block_x)
        .transpose(3, 1, 0, 2)
        .reshape(block_x * block_y, GZ)
    )
    return matmul(returned, table_z).reshape(block_x, block_y, GZ)


def potential_gradient(potential):
    low_x, high_x = edges(potential, "row", 0, 1)
    low_y, high_y = edges(potential, "col", 1, 1)
    wide_x = jnp.concatenate([low_x, potential, high_x], axis=0)
    wide_y = jnp.concatenate([low_y, potential, high_y], axis=1)
    return jnp.stack(
        [
            0.5 * (wide_x[2:] - wide_x[:-2]),
            0.5 * (wide_y[:, 2:] - wide_y[:, :-2]),
            0.5 * (jnp.roll(potential, -1, 2) - jnp.roll(potential, 1, 2)),
        ]
    )


def all_counts(counts, my_column):
    cols_count = lax.axis_size("col")
    if cols_count > 8:
        return lax.all_gather(counts, "col", axis=1, tiled=True).reshape(cols_count)
    column_ids = jnp.arange(cols_count, dtype=jnp.int32)
    result = jnp.where(column_ids == my_column, counts[0, 0], 0)
    for shift in range(1, cols_count):
        pairs = [(i, (i + shift) % cols_count) for i in range(cols_count)]
        arrived = lax.ppermute(counts, "col", pairs)
        sender = (my_column + cols_count - shift) % cols_count
        result = result + jnp.where(column_ids == sender, arrived[0, 0], 0)
    return result


def on_device(fields, counts):
    rows_count = lax.axis_size("row")
    cols_count = lax.axis_size("col")
    my_row = lax.axis_index("row")
    my_column = lax.axis_index("col")
    capacity = fields.shape[0]
    block_x = GX // rows_count
    block_y = GY // cols_count
    lat_x = block_x // PE
    lat_y = GY // PE
    lat_z = GZ // PE
    brick_y = min(PE, block_y)
    per_pencil_y = block_y // brick_y
    repeat_y = max(1, block_y // PE)
    per_peer = capacity // lat_y * repeat_y
    rows = 5 * PE * (brick_y // SUB)
    buffer_rows = cols_count * per_peer
    row_counts = all_counts(counts, my_column)
    starts = jnp.cumsum(row_counts) - row_counts
    column_ids = jnp.arange(cols_count, dtype=jnp.int32)
    own_start = jnp.sum(jnp.where(column_ids == my_column, starts, 0)).astype(jnp.int32)
    own_count = counts[0, 0]
    block_ids = jnp.array(block_of("col"), jnp.int32)
    my_block = jnp.sum(jnp.where(column_ids == my_column, block_ids, 0)).astype(jnp.int32)
    grid_xl = jnp.arange(lat_x, dtype=jnp.int32)[:, None, None]
    grid_w = jnp.arange(per_pencil_y, dtype=jnp.int32)[None, :, None]
    grid_zl = jnp.arange(lat_z, dtype=jnp.int32)[None, None, :]
    pencil_y = (my_block * block_y + grid_w * brick_y) // PE
    curve_pos = (grid_xl * lat_z + grid_zl) * lat_y + pencil_y
    curve_pos = curve_pos.reshape(-1)
    y_flat = jnp.broadcast_to(pencil_y, (lat_x, per_pencil_y, lat_z)).reshape(-1)
    owner = jnp.sum((starts[None, :] <= curve_pos[:, None]).astype(jnp.int32), axis=1) - 1
    owner_start = jnp.sum(
        jnp.where(column_ids[None, :] == owner[:, None], starts[None, :], 0), axis=1
    )
    source_index = (
        owner * per_peer + (curve_pos - owner_start) // lat_y * repeat_y + y_flat % repeat_y
    ).astype(jnp.int32)
    send_buffer = pack_slots(fields, own_start, cols_count, brick_y, lat_y, repeat_y)
    arrived = exchange(send_buffer.reshape(buffer_rows, rows, LANES), "col")
    pencil = gather_bricks(arrived, source_index, lat_x, per_pencil_y, brick_y)
    extended = padded(pencil, (("row", 1), ("col", 2)), 4)
    stepped = advance(extended)
    potential = solve_potential(stepped[0], my_row, my_column, rows_count, cols_count)
    return_buffer = kick_bricks(
        stepped,
        potential_gradient(potential),
        source_index,
        buffer_rows,
        lat_x,
        per_pencil_y,
        brick_y,
    )
    came_back = exchange(return_buffer, "col").reshape(send_buffer.shape)
    return unpack_slots(came_back, own_start, own_count, lat_y)


def solution(mesh):
    return jax.shard_map(
        on_device,
        mesh=mesh,
        in_specs=(P(("row", "col"), None, None), P("row", "col")),
        out_specs=P(("row", "col"), None, None),
        check_vma=False,
    )
```

```python
import functools
import math

import jax
import jax.numpy as jnp
import numpy as np
from jax import lax
from jax.experimental import pallas as pl
from jax.experimental.pallas import tpu as pltpu
from jax.sharding import PartitionSpec as P

PE = 16
GX = 256
GY = 256
GZ = 128
LANES = 128
SUB = 8
TOGETHER = 5
VMEM_BYTES = 56 * 1024 * 1024


gamma_gas = 1.4
speed_bound = 4.0
time_step = 0.03
four_pi_g = 10.0


def ring_order(axis):
    count = lax.axis_size(axis)
    if axis == "col" and count == 8:
        return [0, 2, 4, 6, 7, 5, 3, 1]
    return list(range(count))


def block_of(axis):
    order = ring_order(axis)
    return [order.index(i) for i in range(len(order))]


def shift_pair(axis):
    order = ring_order(axis)
    count = len(order)
    forward = [(order[i], order[(i + 1) % count]) for i in range(count)]
    backward = [(target, source) for source, target in forward]
    return forward, backward


def edges(block, axis, dim, width):
    forward, backward = shift_pair(axis)
    low = lax.ppermute(
        lax.slice_in_dim(block, block.shape[dim] - width, None, axis=dim), axis, forward
    )
    high = lax.ppermute(lax.slice_in_dim(block, 0, width, axis=dim), axis, backward)
    return low, high


def padded(block, sides, width):
    for axis, dim in sides:
        low, high = edges(block, axis, dim, width)
        block = jnp.concatenate([low, block, high], axis=dim)
    return block


def half_flux(state, direction):
    density, momenta, energy = state[0], state[1:4], state[4]
    inverse = 1.0 / density
    velocity = momenta[direction] * inverse
    kinetic = (
        0.5
        * (momenta[0] * momenta[0] + momenta[1] * momenta[1] + momenta[2] * momenta[2])
        * inverse
    )
    pressure = (gamma_gas - 1.0) * (energy - kinetic)
    half_velocity = 0.5 * velocity
    pieces = [0.5 * momenta[direction]]
    for component in range(3):
        term = momenta[component] * half_velocity
        if component == direction:
            term = term + 0.5 * pressure
        pieces.append(term)
    pieces.append((energy + pressure) * half_velocity)
    return pieces


def side_terms(lower_gap, centre, upper_gap, direction):
    left, right = [], []
    for low, mid, high in zip(lower_gap, centre, upper_gap):
        slope = jnp.maximum(jnp.minimum(low, high), 0.0) + jnp.minimum(
            jnp.maximum(low, high), 0.0
        )
        left.append(mid + 0.5 * slope)
        right.append(mid - 0.5 * slope)
    damping = 0.5 * speed_bound
    below = [f + damping * u for f, u in zip(half_flux(left, direction), left)]
    above = [f - damping * u for f, u in zip(half_flux(right, direction), right)]
    return below, above


def step_kernel(ext_ref, out_ref, first_ref, part_ref, last_ref):
    planes = ext_ref.shape[1]
    depth_y = ext_ref.shape[2]
    out_y = out_ref.shape[2]

    def plane(ref, i):
        return [ref[q, i] for q in range(5)]

    def x_terms(ref, i):
        low, mid, high = plane(ref, i - 1), plane(ref, i), plane(ref, i + 1)
        return side_terms(
            [m - l for l, m in zip(low, mid)], mid, [h - m for m, h in zip(mid, high)], 0
        )

    def begin(ref, i):
        before, _ = x_terms(ref, i - 1)
        below, above = x_terms(ref, i)
        for q in range(5):
            last_ref[q] = below[q]
            part_ref[q] = below[q] - above[q] - before[q]

    def change(ref, i):
        below, above = x_terms(ref, i + 1)
        total = []
        for q in range(5):
            total.append(part_ref[q] + above[q])
            part_ref[q] = below[q] - above[q] - last_ref[q]
            last_ref[q] = below[q]
        mid = plane(ref, i)
        for direction, axis, size in ((1, 0, depth_y), (2, 1, LANES)):
            upper_gap = [pltpu.roll(m, size - 1, axis) - m for m in mid]
            lower_gap = [pltpu.roll(g, 1, axis) for g in upper_gap]
            below, above = side_terms(lower_gap, mid, upper_gap, direction)
            total = [
                t + (b - a) + (pltpu.roll(a, size - 1, axis) - pltpu.roll(b, 1, axis))
                for t, b, a in zip(total, below, above)
            ]
        return mid, total

    begin(ext_ref, 2)

    def first_step(i, carry):
        mid, total = change(ext_ref, i)
        for q in range(5):
            first_ref[q, i] = mid[q] - time_step * total[q]
        return carry

    lax.fori_loop(2, planes - 2, first_step, 0)
    begin(first_ref, 4)

    def second_step(i, carry):
        mid, total = change(first_ref, i)
        for q in range(5):
            value = 0.5 * ext_ref[q, i] + 0.5 * (mid[q] - time_step * total[q])
            out_ref[q, i - 4] = pltpu.roll(value, depth_y - 4, 0)[:out_y]
        return carry

    lax.fori_loop(4, planes - 4, second_step, 0)


def advance(extended):
    _, planes, depth_y, depth_z = extended.shape
    out_shape = (5, planes - 8, depth_y - 8, depth_z)
    cells = planes * depth_y * depth_z
    return pl.pallas_call(
        step_kernel,
        out_shape=jax.ShapeDtypeStruct(out_shape, jnp.float32),
        in_specs=[pl.BlockSpec(memory_space=pltpu.VMEM)],
        out_specs=pl.BlockSpec(memory_space=pltpu.VMEM),
        scratch_shapes=[
            pltpu.VMEM((5, planes, depth_y, depth_z), jnp.float32),
            pltpu.VMEM((5, depth_y, depth_z), jnp.float32),
            pltpu.VMEM((5, depth_y, depth_z), jnp.float32),
        ],
        compiler_params=pltpu.CompilerParams(vmem_limit_bytes=VMEM_BYTES),
        cost_estimate=pl.CostEstimate(
            flops=900 * cells, bytes_accessed=40 * cells, transcendentals=0
        ),
        name="gas_step",
    )(extended)


def pack_kernel(start_ref, in_ref, out_ref, rows_ref):
    cols_count, _, repeat_y, rows, _ = out_ref.shape
    lat_y = in_ref.shape[1]
    bricks = cols_count * repeat_y
    per_patch = bricks // lat_y
    halves = 2 // per_patch
    offset = lax.rem(start_ref[0], lat_y)

    for q in range(5):

        def chunk(a, carry):
            for brick in range(per_patch):
                for half in range(halves):
                    lane = pl.multiple_of((2 * a + brick * halves + half) * LANES, LANES)
                    value = pltpu.roll(in_ref[q, :, pl.ds(lane, LANES)], offset, 0)
                    row = brick * rows + (q * PE + a) * halves + half
                    for part in range(lat_y // SUB):
                        rows_ref[
                            pl.ds(
                                part * SUB * per_patch * rows + row,
                                SUB,
                                stride=per_patch * rows,
                            ),
                            :,
                        ] = value[part * SUB : (part + 1) * SUB]
            return carry

        lax.fori_loop(0, PE, chunk, 0, unroll=4)

    for i, block in enumerate(block_of("col")):
        for inner in range(repeat_y):
            out_ref[i, 0, inner] = rows_ref[pl.ds((block * repeat_y + inner) * rows, rows), :]


def pack_slots(fields, own_start, cols_count, brick_y, lat_y, repeat_y):
    capacity = fields.shape[0]
    groups = capacity // lat_y
    rows = 5 * PE * (brick_y // SUB)
    return pl.pallas_call(
        pack_kernel,
        out_shape=jax.ShapeDtypeStruct(
            (cols_count, groups, repeat_y, rows, LANES), jnp.float32
        ),
        grid_spec=pltpu.PrefetchScalarGridSpec(
            num_scalar_prefetch=1,
            grid=(groups,),
            in_specs=[pl.BlockSpec((5, lat_y, PE * PE * PE), lambda g, s: (0, g, 0))],
            out_specs=pl.BlockSpec(
                (cols_count, 1, repeat_y, rows, LANES), lambda g, s: (0, g, 0, 0, 0)
            ),
            scratch_shapes=[pltpu.VMEM((cols_count * repeat_y * rows, LANES), jnp.float32)],
        ),
        compiler_params=pltpu.CompilerParams(vmem_limit_bytes=VMEM_BYTES),
        name="pack_slots",
    )(own_start.reshape(1), fields.transpose(1, 0, 2))


def unpack_kernel(info_ref, in_ref, out_ref, rows_ref):
    cols_count, _, repeat_y, rows, _ = in_ref.shape
    lat_y = out_ref.shape[1]
    bricks = cols_count * repeat_y
    per_patch = bricks // lat_y
    halves = 2 // per_patch
    offset = lax.rem(lat_y - lax.rem(info_ref[0], lat_y), lat_y)
    for i, block in enumerate(block_of("col")):
        for inner in range(repeat_y):
            rows_ref[pl.ds((block * repeat_y + inner) * rows, rows), :] = in_ref[i, 0, inner]
    slot = pl.program_id(0) * lat_y + lax.broadcasted_iota(jnp.int32, (lat_y, LANES), 0)
    live = slot < info_ref[1]

    for q in range(5):

        def chunk(a, carry):
            for brick in range(per_patch):
                for half in range(halves):
                    lane = pl.multiple_of((2 * a + brick * halves + half) * LANES, LANES)
                    row = brick * rows + (q * PE + a) * halves + half
                    value = jnp.concatenate(
                        [
                            rows_ref[
                                pl.ds(
                                    part * SUB * per_patch * rows + row,
                                    SUB,
                                    stride=per_patch * rows,
                                ),
                                :,
                            ]
                            for part in range(lat_y // SUB)
                        ],
                        axis=0,
                    )
                    value = pltpu.roll(value, offset, 0)
                    out_ref[q, :, pl.ds(lane, LANES)] = jnp.where(live, value, 0.0)
            return carry

        lax.fori_loop(0, PE, chunk, 0, unroll=4)


def unpack_slots(arrived, own_start, own_count, lat_y):
    cols_count, groups, repeat_y, rows, _ = arrived.shape
    out = pl.pallas_call(
        unpack_kernel,
        out_shape=jax.ShapeDtypeStruct((5, groups * lat_y, PE * PE * PE), jnp.float32),
        grid_spec=pltpu.PrefetchScalarGridSpec(
            num_scalar_prefetch=1,
            grid=(groups,),
            in_specs=[
                pl.BlockSpec(
                    (cols_count, 1, repeat_y, rows, LANES), lambda g, s: (0, g, 0, 0, 0)
                )
            ],
            out_specs=pl.BlockSpec((5, lat_y, PE * PE * PE), lambda g, s: (0, g, 0)),
            scratch_shapes=[pltpu.VMEM((cols_count * repeat_y * rows, LANES), jnp.float32)],
        ),
        compiler_params=pltpu.CompilerParams(vmem_limit_bytes=VMEM_BYTES),
        name="unpack_slots",
    )(jnp.stack([own_start, own_count]), arrived)
    return out.transpose(1, 0, 2)


def swap_many(many):
    lane = lax.broadcasted_iota(jnp.int32, (SUB, LANES), 1)
    step = 1
    while step < GZ // PE:
        shift = step * PE
        low = (lane // shift) % 2 == 0
        result = []
        for values in many:
            swapped = list(values)
            for i, one in enumerate(values):
                if i & step == 0:
                    two = values[i | step]
                    swapped[i] = jnp.where(low, one, pltpu.roll(two, shift, 1))
                    swapped[i | step] = jnp.where(low, pltpu.roll(one, LANES - shift, 1), two)
            result.append(swapped)
        many = result
        step *= 2
    return many


def gather_kernel(index_ref, *refs):
    lat_z = GZ // PE
    in_refs, out_ref, rows_ref = refs[:lat_z], refs[lat_z], refs[lat_z + 1]
    brick_y = out_ref.shape[3]
    groups = in_refs[0].shape[1] // SUB

    def regroup(n, carry):
        firsts = [n * TOGETHER + m for m in range(TOGETHER)]
        values = [
            [ref[0, pl.ds(pl.multiple_of(m * SUB, SUB), SUB), :] for ref in in_refs]
            for m in firsts
        ]
        for m, swapped in zip(firsts, swap_many(values)):
            for b in range(SUB):
                rows_ref[pl.ds(m * (SUB * SUB) + b, SUB, stride=SUB), :] = swapped[b]
        return carry

    lax.fori_loop(0, groups // TOGETHER, regroup, 0)
    for q in range(5):
        for a in range(PE):
            out_ref[q, a, 0] = rows_ref[pl.ds((q * PE + a) * brick_y, brick_y), :]


def gather_bricks(arrived, source_index, lat_x, per_pencil_y, brick_y):
    lat_z = GZ // PE
    rows = arrived.shape[1]

    def picked(zl):
        return lambda i, w, index: (index[(i * per_pencil_y + w) * lat_z + zl], 0, 0)

    out = pl.pallas_call(
        gather_kernel,
        out_shape=jax.ShapeDtypeStruct(
            (5, lat_x * PE, per_pencil_y, brick_y, LANES), jnp.float32
        ),
        grid_spec=pltpu.PrefetchScalarGridSpec(
            num_scalar_prefetch=1,
            grid=(lat_x, per_pencil_y),
            in_specs=[pl.BlockSpec((1, rows, LANES), picked(zl)) for zl in range(lat_z)],
            out_specs=pl.BlockSpec(
                (5, PE, 1, brick_y, LANES), lambda i, w, index: (0, i, w, 0, 0)
            ),
            scratch_shapes=[pltpu.VMEM((rows * SUB, LANES), jnp.float32)],
        ),
        compiler_params=pltpu.CompilerParams(vmem_limit_bytes=VMEM_BYTES),
        name="gather_bricks",
    )(source_index, *([arrived] * lat_z))
    return out.reshape(5, lat_x * PE, per_pencil_y * brick_y, GZ)


def kick_kernel(index_ref, state_ref, gradient_ref, out_ref, rows_ref, brick_ref, sems):
    lat_z = GZ // PE
    brick_y = state_ref.shape[3]
    groups = brick_ref.shape[1] // SUB
    at_grid = (pl.program_id(0) * pl.num_programs(1) + pl.program_id(1)) * lat_z

    def kick(a, carry):
        density = state_ref[0, a, 0]
        momenta = [state_ref[1 + d, a, 0] for d in range(3)]
        slopes = [gradient_ref[d, a, 0] for d in range(3)]
        work = momenta[0] * slopes[0] + momenta[1] * slopes[1] + momenta[2] * slopes[2]
        pieces = [density]
        for d in range(3):
            pieces.append(momenta[d] - time_step * density * slopes[d])
        pieces.append(state_ref[4, a, 0] - time_step * work)
        for q in range(5):
            at = pl.multiple_of((q * PE + a) * brick_y, SUB)
            rows_ref[pl.ds(at, brick_y), :] = pieces[q]
        return carry

    lax.fori_loop(0, PE, kick, 0, unroll=4)

    def regroup(n, carry):
        firsts = [n * TOGETHER + m for m in range(TOGETHER)]
        values = [
            [rows_ref[pl.ds(m * (SUB * SUB) + b, SUB, stride=SUB), :] for b in range(SUB)]
            for m in firsts
        ]
        for m, swapped in zip(firsts, swap_many(values)):
            for zl in range(lat_z):
                brick_ref[zl, pl.ds(pl.multiple_of(m * SUB, SUB), SUB), :] = swapped[zl]
        return carry

    lax.fori_loop(0, groups // TOGETHER, regroup, 0)
    copies = [
        pltpu.make_async_copy(
            brick_ref.at[zl], out_ref.at[index_ref[at_grid + zl]], sems.at[zl]
        )
        for zl in range(lat_z)
    ]
    for copy in copies:
        copy.start()
    for copy in copies:
        copy.wait()


def kick_bricks(stepped, gradient, source_index, buffer_rows, lat_x, per_pencil_y, brick_y):
    lat_z = GZ // PE
    rows = 5 * PE * (brick_y // SUB)
    shape = (lat_x * PE, per_pencil_y, brick_y, GZ)

    def block(count):
        return pl.BlockSpec((count, PE, 1, brick_y, GZ), lambda i, w, index: (0, i, w, 0, 0))

    return pl.pallas_call(
        kick_kernel,
        out_shape=jax.ShapeDtypeStruct((buffer_rows, rows, LANES), jnp.float32),
        grid_spec=pltpu.PrefetchScalarGridSpec(
            num_scalar_prefetch=1,
            grid=(lat_x, per_pencil_y),
            in_specs=[block(5), block(3)],
            out_specs=pl.BlockSpec(memory_space=pl.ANY),
            scratch_shapes=[
                pltpu.VMEM((rows * SUB, LANES), jnp.float32),
                pltpu.VMEM((lat_z, rows, LANES), jnp.float32),
                pltpu.SemaphoreType.DMA((lat_z,)),
            ],
        ),
        compiler_params=pltpu.CompilerParams(vmem_limit_bytes=VMEM_BYTES),
        name="kick_bricks",
    )(source_index, stepped.reshape((5,) + shape), gradient.reshape((3,) + shape))


def lap_eigen(wave, length):
    return 2.0 * jnp.cos(2.0 * math.pi / length * wave) - 2.0


def hartley(length):
    indices = np.arange(length)
    angles = 2.0 * np.pi / length * (indices[:, None] * indices[None, :] % length)
    return jnp.asarray((np.cos(angles) + np.sin(angles)).astype(np.float32))


def matmul(a, b):
    return jnp.matmul(a, b, precision=lax.Precision.HIGHEST)


def exchange(packed, axis):
    return lax.all_to_all(packed, axis, split_axis=0, concat_axis=0, tiled=True)


def solve_potential(density, my_row, my_column, rows_count, cols_count):
    block_x, block_y, _ = density.shape
    rows_y = GY // rows_count
    cols_z = GZ // cols_count
    table_x, table_y, table_z = hartley(GX), hartley(GY), hartley(GZ)
    table_y = jnp.concatenate(
        [table_y[block * block_y : (block + 1) * block_y] for block in block_of("col")]
    )
    along = lax.optimization_barrier(
        matmul(density.reshape(block_x * block_y, GZ), table_z)
    )
    packed = along.reshape(block_x, block_y, cols_count, cols_z).transpose(2, 1, 3, 0)
    mid = exchange(packed.reshape(GY, cols_z * block_x), "col")
    spectrum = exchange(matmul(table_y.T, mid), "row")
    spectrum = (
        spectrum.reshape(rows_count, rows_y, cols_z, block_x)
        .transpose(1, 2, 0, 3)
        .reshape(rows_y * cols_z, GX)
    )
    spectrum = matmul(spectrum, table_x)
    index_x = jnp.arange(GX, dtype=jnp.int32)
    index_y = my_row * rows_y + jnp.arange(rows_y, dtype=jnp.int32)
    index_z = my_column * cols_z + jnp.arange(cols_z, dtype=jnp.int32)
    eigen = (
        lap_eigen(index_x.astype(jnp.float32), GX)[None, None, :]
        + lap_eigen(index_y.astype(jnp.float32), GY)[:, None, None]
        + lap_eigen(index_z.astype(jnp.float32), GZ)[None, :, None]
    )
    zero_mode = (
        (index_x == 0)[None, None, :]
        & (index_y == 0)[:, None, None]
        & (index_z == 0)[None, :, None]
    )
    scale = 1.0 / (GX * GY * GZ)
    green = jnp.where(
        zero_mode, 0.0, four_pi_g * scale / jnp.where(zero_mode, -1.0, eigen)
    ).reshape(rows_y * cols_z, GX)
    back = matmul(spectrum * green, table_x)
    packed = back.reshape(rows_y, cols_z, rows_count, block_x).transpose(2, 0, 1, 3)
    mid = exchange(packed.reshape(GY, cols_z * block_x), "row")
    returned = exchange(matmul(table_y, mid), "col")
    returned = (
        returned.reshape(cols_count, block_y, cols_z, block_x)
        .transpose(3, 1, 0, 2)
        .reshape(block_x * block_y, GZ)
    )
    return matmul(returned, table_z).reshape(block_x, block_y, GZ)


def potential_gradient(potential):
    low_x, high_x = edges(potential, "row", 0, 1)
    low_y, high_y = edges(potential, "col", 1, 1)
    wide_x = jnp.concatenate([low_x, potential, high_x], axis=0)
    wide_y = jnp.concatenate([low_y, potential, high_y], axis=1)
    return jnp.stack(
        [
            0.5 * (wide_x[2:] - wide_x[:-2]),
            0.5 * (wide_y[:, 2:] - wide_y[:, :-2]),
            0.5 * (jnp.roll(potential, -1, 2) - jnp.roll(potential, 1, 2)),
        ]
    )


def on_device(fields, counts):
    rows_count = lax.axis_size("row")
    cols_count = lax.axis_size("col")
    my_row = lax.axis_index("row")
    my_column = lax.axis_index("col")
    capacity = fields.shape[0]
    block_x = GX // rows_count
    block_y = GY // cols_count
    lat_x = block_x // PE
    lat_y = GY // PE
    lat_z = GZ // PE
    brick_y = min(PE, block_y)
    per_pencil_y = block_y // brick_y
    repeat_y = max(1, block_y // PE)
    per_peer = capacity // lat_y * repeat_y
    rows = 5 * PE * (brick_y // SUB)
    buffer_rows = cols_count * per_peer
    row_counts = lax.all_gather(counts, "col", axis=1, tiled=True).reshape(cols_count)
    starts = jnp.cumsum(row_counts) - row_counts
    column_ids = jnp.arange(cols_count, dtype=jnp.int32)
    own_start = jnp.sum(jnp.where(column_ids == my_column, starts, 0)).astype(jnp.int32)
    own_count = counts[0, 0]
    block_ids = jnp.array(block_of("col"), jnp.int32)
    my_block = jnp.sum(jnp.where(column_ids == my_column, block_ids, 0)).astype(jnp.int32)
    grid_xl = jnp.arange(lat_x, dtype=jnp.int32)[:, None, None]
    grid_w = jnp.arange(per_pencil_y, dtype=jnp.int32)[None, :, None]
    grid_zl = jnp.arange(lat_z, dtype=jnp.int32)[None, None, :]
    pencil_y = (my_block * block_y + grid_w * brick_y) // PE
    curve_pos = (grid_xl * lat_z + grid_zl) * lat_y + pencil_y
    curve_pos = curve_pos.reshape(-1)
    y_flat = jnp.broadcast_to(pencil_y, (lat_x, per_pencil_y, lat_z)).reshape(-1)
    owner = jnp.sum((starts[None, :] <= curve_pos[:, None]).astype(jnp.int32), axis=1) - 1
    owner_start = jnp.sum(
        jnp.where(column_ids[None, :] == owner[:, None], starts[None, :], 0), axis=1
    )
    source_index = (
        owner * per_peer + (curve_pos - owner_start) // lat_y * repeat_y + y_flat % repeat_y
    ).astype(jnp.int32)
    send_buffer = pack_slots(fields, own_start, cols_count, brick_y, lat_y, repeat_y)
    arrived = exchange(send_buffer.reshape(buffer_rows, rows, LANES), "col")
    pencil = gather_bricks(arrived, source_index, lat_x, per_pencil_y, brick_y)
    extended = padded(pencil, (("row", 1), ("col", 2)), 4)
    stepped = advance(extended)
    potential = solve_potential(stepped[0], my_row, my_column, rows_count, cols_count)
    return_buffer = kick_bricks(
        stepped,
        potential_gradient(potential),
        source_index,
        buffer_rows,
        lat_x,
        per_pencil_y,
        brick_y,
    )
    came_back = exchange(return_buffer, "col").reshape(send_buffer.shape)
    return unpack_slots(came_back, own_start, own_count, lat_y)


def solution(mesh):
    return jax.shard_map(
        on_device,
        mesh=mesh,
        in_specs=(P(("row", "col"), None, None), P("row", "col")),
        out_specs=P(("row", "col"), None, None),
        check_vma=False,
    )
```
